128 devices in a mesh: sub: 2 (over x_hi), dp: 16 (over z, y), mp: 4 (over x_lo, core).
Axes of the slice: x: 4 (x_hi: 2, x_lo: 2; x = x_hi * 2 + x_lo), y: 4, z: 4, core: 2. Of those that a mesh axis runs over, the one named last changes fastest.
Arguments:
- features: bfloat16 [16384, 1024], P(('sub', 'dp', 'mp')), may hold values from -6 to 6
- teacher: bfloat16 [16384, 1024], P(('sub', 'dp', 'mp')), may hold values from -6 to 6
- proj: bfloat16 [1024, 1024], replicated, may hold values from -0.1875 to 0.1875
Outputs:
- feature_grad: float32 [16384, 1024], P(('sub', 'dp', 'mp'))
The draws below stay inside these ranges and needn't reach their ends.
All inputs are finite; a program needn't handle non-finite values.
Results may differ from the reference program's by a relative error of at most 0.0095.
Values may be sent and summed in bfloat16 or wider, within the bound.
A program may use at most 128 MiB of HBM per device.

```python
import jax
import jax.numpy as jnp
from jax import lax

E = 1024
W = 1024
BATCH = 16384


def draw_features(key, part):
    key = jax.random.fold_in(key, 11)
    base = jax.random.normal(key, (BATCH, W), jnp.float32)
    return jnp.clip(base, -6.0, 6.0).astype(jnp.bfloat16)


def draw_teacher(key, part):
    key = jax.random.fold_in(key, 12)
    base = jax.random.normal(key, (BATCH, E), jnp.float32)
    return jnp.clip(base, -6.0, 6.0).astype(jnp.bfloat16)


def normal_values(key, extent, width, bound, kind=jnp.bfloat16):
    values = width * jax.random.normal(key, extent, jnp.float32)
    return jnp.clip(values, min=-bound, max=bound).astype(kind)


def setup_inputs(seed: int = 0) -> dict:
    arg_keys = jax.random.split(jax.random.key(seed), 4)
    features = draw_features(jax.random.fold_in(arg_keys[3], 71), 0)
    teacher = draw_teacher(jax.random.fold_in(arg_keys[3], 71), 0)
    proj = normal_values(arg_keys[2], (W, E), W ** -0.5, 0.1875)
    return {"features": features, "teacher": teacher, "proj": proj}


logit_scale = 100.0
epsilon = 1e-06

def unit_rows(values):
    norm_rows = jnp.sqrt(lax.optimization_barrier(jnp.sum(values * values, axis=1, keepdims=True)) + epsilon)
    return (values / norm_rows, norm_rows)

def reference(features, teacher, proj):
    student = jnp.dot(features.astype(jnp.float32), proj.astype(jnp.float32), preferred_element_type=jnp.float32)
    student_unit, student_norm = unit_rows(student)
    student_rows = student_unit.astype(jnp.bfloat16).astype(jnp.float32)
    teacher_rows = unit_rows(teacher.astype(jnp.float32))[0].astype(jnp.bfloat16).astype(jnp.float32)
    total_rows = student_rows.shape[0]
    block_count = 16
    span = total_rows // block_count
    indices = jnp.arange(block_count, dtype=jnp.int32)

    def scores(index):
        start = index * span
        s_block = lax.dynamic_slice_in_dim(student_rows, start, span, 0)
        t_block = lax.dynamic_slice_in_dim(teacher_rows, start, span, 0)
        s_score = logit_scale * jnp.dot(s_block, student_rows.T, preferred_element_type=jnp.float32)
        t_score = logit_scale * jnp.dot(t_block, teacher_rows.T, preferred_element_type=jnp.float32)
        row_ids = start + jnp.arange(span, dtype=jnp.int32)[:, None]
        column_ids = jnp.arange(total_rows, dtype=jnp.int32)[None, :]
        return (s_score, t_score, row_ids == column_ids)

    def partial_totals(score, diagonal_mask):
        row_top = lax.optimization_barrier(jnp.max(jnp.where(diagonal_mask, -jnp.inf, score), axis=1))
        row_sum = lax.optimization_barrier(jnp.sum(jnp.where(diagonal_mask, 0.0, jnp.exp(score - row_top[:, None])), axis=1))
        return (row_top, row_sum)

    def block_totals(index):
        s_score, t_score, diagonal_mask = scores(index)
        s_top, s_sum = partial_totals(s_score, diagonal_mask)
        t_top, t_sum = partial_totals(t_score, diagonal_mask)
        return (s_top, s_sum, t_top, t_sum)
    totals = lax.map(block_totals, indices)
    s_top, s_sum, t_top, t_sum = [part.reshape(total_rows) for part in totals]

    def block_term(index):
        s_score, t_score, diagonal_mask = scores(index)
        start = index * span
        s_top_rows = lax.dynamic_slice_in_dim(s_top, start, span, 0)[:, None]
        s_sum_rows = lax.dynamic_slice_in_dim(s_sum, start, span, 0)[:, None]
        t_top_rows = lax.dynamic_slice_in_dim(t_top, start, span, 0)[:, None]
        t_sum_rows = lax.dynamic_slice_in_dim(t_sum, start, span, 0)[:, None]
        own_weight = jnp.where(diagonal_mask, 0.0, jnp.exp(s_score - s_top_rows) / s_sum_rows - jnp.exp(t_score - t_top_rows) / t_sum_rows)
        cross_weight = jnp.where(diagonal_mask, 0.0, jnp.exp(s_score - s_top[None, :]) / s_sum[None, :] - jnp.exp(t_score - t_top[None, :]) / t_sum[None, :])
        own_weight = own_weight.astype(jnp.bfloat16).astype(jnp.float32)
        cross_weight = cross_weight.astype(jnp.bfloat16).astype(jnp.float32)
        return jnp.dot(own_weight, student_rows, preferred_element_type=jnp.float32) + jnp.dot(cross_weight, student_rows, preferred_element_type=jnp.float32)
    term = lax.map(block_term, indices).reshape(total_rows, student_rows.shape[1])
    grad = logit_scale * term
    along = lax.optimization_barrier(jnp.sum(student_unit * grad, axis=1, keepdims=True))
    d_student = ((grad - student_unit * along) / student_norm).astype(jnp.bfloat16)
    return jnp.dot(d_student.astype(jnp.float32), proj.astype(jnp.float32).T, preferred_element_type=jnp.float32)
```

```python
import functools

import jax
import jax.numpy as jnp
from jax import lax
from jax.experimental import pallas as pl
from jax.experimental.pallas import tpu as pltpu
from jax.sharding import PartitionSpec as P

MESH = pl.DeviceIdType.MESH
logit_scale = 100.0
epsilon = 1e-06
log2e = 1.4426950408889634
NEG = -1e30

PLACE = (
    (2, 3, 0), (1, 3, 0), (3, 3, 0), (0, 3, 0), (0, 0, 3), (0, 3, 1), (0, 1, 3), (0, 3, 2),
    (0, 0, 0), (0, 0, 1), (0, 1, 0), (0, 0, 2), (0, 1, 2),
)
SLOTS = 13
OWN = 8
COLS = 5
SHARE = ((0.5, 1.0, 1.0, 1.0, 0.5), (1.0, 1.0, 0.5, 1.0, 0.5))
FROM = (
    ((1, 3, 3, 8, 8, 3, 4, 11, -1, 8, 8, 9, 6), (2, 3, 3, 8, 8, 9, 4, 5, -1, 8, 8, 9, 11)),
    ((1, 3, 3, 8, 8, 9, 4, 5, -1, 8, 8, 4, 11), (2, 3, 3, 8, 8, 9, 10, 11, -1, 8, 8, 4, 6)),
)
INTO = (3, 3, 3, 8, 8, 9, 4, 11, -1, 8, 8, 8, 11)
T, S = 0, 1


def step(a, b):
    return tuple((p - q) % 4 for p, q in zip(a, b))


def partner_places():
    places = set()
    for place in PLACE:
        places |= {place, step((0, 0, 0), place)}
    for slot in range(SLOTS):
        for kind in (T, S):
            for core in (0, 1):
                if FROM[kind][core][slot] >= 0:
                    move = step(PLACE[FROM[kind][core][slot]], PLACE[slot])
                    places |= {move, step((0, 0, 0), move)}
        if INTO[slot] >= 0:
            move = step(PLACE[slot], PLACE[INTO[slot]])
            places |= {move, step((0, 0, 0), move)}
    places.discard((0, 0, 0))
    return sorted(places)


PARTNERS = partner_places()


def rows_of(slot, count=1):
    return pl.ds(slot * 256, count * 256)


def kernel(
    features, teacher, proj, out,
    s_rows, t_rows, s_score, t_score, weight, top_parts, sum_parts, col_top, col_sum,
    stat_out, stat_in, lse_out, lse_in, lse_rows, part_a, part_b, stage, joined,
    unit, norm,
    g_send, g_recv, c_send, c_recv, st_send, st_recv, l_send, l_recv,
    pa_send, pa_recv, pb_send, pb_recv, r_send, r_recv,
):
    sub, dp, mp = lax.axis_index("sub"), lax.axis_index("dp"), lax.axis_index("mp")
    x, y, z, core = sub * 2 + mp // 2, dp % 4, dp // 4, mp % 2
    other = 1 - core
    half = core * 128
    sibling = (sub, dp, (mp // 2) * 2 + other)
    rows_buf = (t_rows, s_rows)
    score_buf = (t_score, s_score)

    def device(move, to_core):
        ax, ay, az = (x + move[0]) % 4, (y + move[1]) % 4, (z + move[2]) % 4
        return (ax // 2, az * 4 + ay, (ax % 2) * 2 + to_core)

    barrier = pltpu.get_barrier_semaphore()
    for move in PARTNERS:
        for to_core in (0, 1):
            pl.semaphore_signal(barrier, inc=1, device_id=device(move, to_core), device_id_type=MESH)
    pl.semaphore_signal(barrier, inc=1, device_id=sibling, device_id_type=MESH)

    def remote(src, dst, send, recv, target):
        return pltpu.make_async_remote_copy(
            src_ref=src, dst_ref=dst, send_sem=send, recv_sem=recv, device_id=target, device_id_type=MESH
        )

    def half_rows(kind, slot, which):
        return rows_buf[kind].at[pl.ds(slot * 256 + which, 128)]

    def row_copy(kind, src_slot, slot):
        move = step(PLACE[src_slot], PLACE[slot])
        return remote(
            half_rows(kind, src_slot, half), half_rows(kind, slot, half),
            g_send.at[kind, slot], g_recv.at[kind, slot], device(move, core),
        )

    def side_copy(kind, slot, which):
        piece = half_rows(kind, slot, which)
        return remote(piece, piece, c_send.at[kind, slot], c_recv.at[kind, slot], sibling)

    def to_side(kind, slot):
        if slot < 4:
            side_copy(kind, slot, half).start()
        else:
            @pl.when(core == (1 if slot < OWN else 0))
            def _():
                side_copy(kind, slot, half).start()

    def forward(kind, slot):
        for which in (0, 1):
            children = [d for d in range(SLOTS) if FROM[kind][which][d] == slot]
            if children:
                @pl.when(core == which)
                def _(children=children):
                    for child in children:
                        row_copy(kind, slot, child).start()
        to_side(kind, slot)

    def arrive(kind, slot):
        row_copy(kind, OWN, slot).wait_recv()
        forward(kind, slot)

    def side_wait(kind, *slots):
        for slot in slots:
            if slot < 4:
                side_copy(kind, slot, 128 - half).wait_recv()
            else:
                @pl.when(core == (0 if slot < OWN else 1))
                def _(slot=slot):
                    side_copy(kind, slot, 128 - half).wait_recv()

    own_rows = pl.ds(OWN * 256 + half, 128)
    values = teacher[...].astype(jnp.float32)
    t_rows[own_rows, :] = (
        values / jnp.sqrt(jnp.sum(values * values, axis=1, keepdims=True) + epsilon)
    ).astype(jnp.bfloat16)

    pl.semaphore_wait(barrier, 2 * len(PARTNERS) + 1)
    forward(T, OWN)

    student = jnp.dot(features[...], proj[...], preferred_element_type=jnp.float32)
    length = jnp.sqrt(jnp.sum(student * student, axis=1, keepdims=True) + epsilon)
    student = student / length
    unit[...] = student
    norm[...] = jnp.broadcast_to(length, norm.shape)
    s_rows[own_rows, :] = student.astype(jnp.bfloat16)
    forward(S, OWN)

    for kind in (T, S):
        top_parts[kind] = jnp.full(top_parts.shape[1:], NEG, jnp.float32)
        sum_parts[kind] = jnp.zeros(sum_parts.shape[1:], jnp.float32)
        col_top[kind] = jnp.full(col_top.shape[1:], NEG, jnp.float32)
        col_sum[kind] = jnp.zeros(col_sum.shape[1:], jnp.float32)

    col_base = 3 + COLS * core
    pair_dims = (((1,), (1,)), ((), ()))
    lanes = lax.broadcasted_iota(jnp.int32, (256, 128), 1)

    def scores(kind, a0, na, j0, nj):
        buf, score = rows_buf[kind], score_buf[kind]

        def column(i, carry):
            j = j0 + i
            cols = buf[pl.ds(pl.multiple_of((col_base + j) * 256, 256), 256), :]
            score[pl.ds(a0 * 256, na * 256), pl.ds(pl.multiple_of(j * 256, 256), 256)] = (
                lax.dot_general(
                    buf[pl.ds(a0 * 256, na * 256), :], cols, pair_dims, preferred_element_type=jnp.float32
                ) * (logit_scale * log2e)
            )
            return carry

        lax.fori_loop(0, nj, column, 0)
        if a0 <= 3 < a0 + na and j0 == 0:
            @pl.when(core == 0)
            def _():
                tile = score[pl.ds(768, 256), pl.ds(0, 256)]
                row = lax.broadcasted_iota(jnp.int32, (256, 256), 0)
                col = lax.broadcasted_iota(jnp.int32, (256, 256), 1)
                score[pl.ds(768, 256), pl.ds(0, 256)] = jnp.where(row == col, NEG, tile)

        def totals(i, carry):
            a, j = a0 + i // nj, j0 + i % nj
            rows = pl.ds(pl.multiple_of(a * 256, 256), 256)
            cols = pl.ds(pl.multiple_of(j * 256, 256), 256)
            tile = score[rows, cols]
            top = jnp.max(tile, axis=1, keepdims=True)
            total = jnp.sum(jnp.exp2(tile - top), axis=1, keepdims=True)
            here = lanes == j
            top_parts[kind, rows, :] = jnp.where(here, top, top_parts[kind, rows, :])
            sum_parts[kind, rows, :] = jnp.where(here, total, sum_parts[kind, rows, :])
            top = jnp.max(tile, axis=0, keepdims=True)
            total = jnp.sum(jnp.exp2(tile - top), axis=0, keepdims=True)
            col_top[kind, pl.ds(a, 1), cols] = top
            col_sum[kind, pl.ds(a, 1), cols] = total
            return carry

        lax.fori_loop(0, na * nj, totals, 0)

    for kind, slot in ((T, 3), (T, 9), (T, 4), (T, 10), (S, 3), (S, 9), (S, 4), (S, 10)):
        arrive(kind, slot)
    for kind, slot in ((T, 1), (T, 2), (S, 1), (S, 2)):
        arrive(kind, slot)
    for kind in (T, S):
        side_wait(kind, 3, 4, 8, 9)
        scores(kind, 3, 1, 0, 2)
    for kind, slot in ((T, 6), (T, 11), (T, 5), (S, 6), (S, 11), (S, 5)):
        arrive(kind, slot)
    for kind in (T, S):
        side_wait(kind, 1, 2)
        scores(kind, 1, 2, 0, 2)
    for kind, slot in ((T, 0), (S, 0)):
        arrive(kind, slot)
    for kind in (T, S):
        side_wait(kind, 5, 6, 10, 11)
        scores(kind, 1, 3, 2, 2)
    for kind, slot in ((T, 7), (T, 12), (S, 7), (S, 12)):
        arrive(kind, slot)
    for kind in (T, S):
        side_wait(kind, 0)
        scores(kind, 0, 1, 0, 4)
    for kind in (T, S):
        side_wait(kind, 7, 12)
        scores(kind, 0, 4, 4, 1)

    def share(j):
        return jnp.where(core == 0, SHARE[0][j], SHARE[1][j]).astype(jnp.float32)

    share_lanes = jnp.zeros((256, 128), jnp.float32)
    for j in range(COLS):
        share_lanes = jnp.where(lanes == j, share(j), share_lanes)

    for a in range(4):
        rows = pl.ds(a * 256, 256)
        packed = jnp.zeros((256, 128), jnp.float32)
        for kind in (T, S):
            parts = top_parts[kind, rows, :]
            top = jnp.max(parts, axis=1, keepdims=True)
            total = jnp.sum(
                sum_parts[kind, rows, :] * share_lanes * jnp.exp2(parts - top), axis=1, keepdims=True
            )
            packed = jnp.where(lanes == 2 * kind, top, packed)
            packed = jnp.where(lanes == 2 * kind + 1, total, packed)
        turned = packed.T
        stat_out[a, 0] = turned[0:8, 0:128]
        stat_out[a, 1] = turned[0:8, 128:256]
    for j in range(COLS):
        cols = pl.ds(j * 256, 256)
        lines = []
        for kind in (T, S):
            parts = col_top[kind, :, cols]
            top = jnp.max(parts, axis=0, keepdims=True)
            total = jnp.sum(col_sum[kind, :, cols] * jnp.exp2(parts - top), axis=0, keepdims=True)
            lines += [top, total * share(j)]
        lines.append(jnp.zeros((4, 256), jnp.float32))
        lines = jnp.concatenate(lines, axis=0)
        stat_out[4 + j, 0] = lines[:, 0:128]
        stat_out[4 + j, 1] = lines[:, 128:256]

    def place_at(index, of_core):
        if index < 4:
            return PLACE[index]
        first, second = PLACE[index - 1], PLACE[index + 4]
        return tuple(jnp.where(of_core == 0, p, q) for p, q in zip(first, second))

    def back(move):
        return tuple(4 - m for m in move)

    def stat_copy(index, to_half):
        return remote(
            stat_out.at[index, to_half], stat_in.at[core * 9 + index],
            st_send.at[index * 2 + to_half], st_recv.at[core * 9 + index],
            device(place_at(index, core), to_half),
        )

    def unless_own(index, to_half, action, instead=None):
        if index == 4 and to_half == 1:
            pl.when(core == 0)(action)
            if instead is not None:
                pl.when(core == 1)(instead)
        else:
            action()

    def keep_stat():
        stat_in[9 + 4] = stat_out[4, 1]

    for index in range(9):
        for to_half in (0, 1):
            unless_own(index, to_half, lambda: stat_copy(index, to_half).start(), keep_stat)

    def stat_arrival(source):
        return remote(
            stat_out.at[0, 0], stat_in.at[source], st_send.at[0], st_recv.at[source], sibling
        )

    for source in range(18):
        if source == 9 + 4:
            pl.when(core == 0)(lambda: stat_arrival(13).wait_recv())
        else:
            stat_arrival(source).wait_recv()

    lines = []
    for kind in (T, S):
        tops = stat_in[:, 2 * kind, :]
        top = jnp.max(tops, axis=0, keepdims=True)
        total = jnp.sum(stat_in[:, 2 * kind + 1, :] * jnp.exp2(tops - top), axis=0, keepdims=True)
        lines.append(top + jnp.log(total) * log2e)
    lines.append(jnp.zeros((6, 128), jnp.float32))
    lse_out[...] = jnp.concatenate(lines, axis=0)

    def lse_copy(of_core, index):
        return remote(
            lse_out, lse_in.at[index, core],
            l_send.at[of_core * 9 + index], l_recv.at[index * 2 + core],
            device(back(place_at(index, jnp.int32(of_core)) if index < 4 else PLACE[index - 1 + 5 * of_core]), of_core),
        )

    def lse_arrival(index, from_half):
        return remote(
            lse_out, lse_in.at[index, from_half], l_send.at[0], l_recv.at[index * 2 + from_half], sibling
        )

    def keep_lse():
        lse_in[4, 1] = lse_out[...]

    for index in range(9):
        for of_core in (0, 1):
            if index == 4 and of_core == 1:
                pl.when(core == 0)(lambda: lse_copy(1, 4).start())
                pl.when(core == 1)(keep_lse)
            else:
                lse_copy(of_core, index).start()
    for index in range(9):
        for from_half in (0, 1):
            unless_own(index, from_half, lambda: lse_arrival(index, from_half).wait_recv())

    for a in range(4):
        lines = jnp.concatenate(
            [
                jnp.concatenate([lse_in[a, 0], lse_in[a, 1]], axis=1),
                jnp.zeros((120, 256), jnp.float32),
            ],
            axis=0,
        ).T
        for kind in (T, S):
            lse_rows[kind, pl.ds(a * 256, 256), :] = jnp.broadcast_to(lines[:, kind:kind + 1], (256, 128))

    def weights(a):
        for j in range(COLS):
            for side in (0, 1):
                def chunk(i, carry):
                    rows = pl.ds(pl.multiple_of(a * 256 + i * 64, 64), 64)
                    cols = pl.ds(j * 256 + side * 128, 128)
                    s_tile, t_tile = s_score[rows, cols], t_score[rows, cols]
                    value = (
                        jnp.exp2(s_tile - lse_rows[S, rows, :])
                        + jnp.exp2(s_tile - lse_in[4 + j, side, S:S + 1, :])
                        - jnp.exp2(t_tile - lse_rows[T, rows, :])
                        - jnp.exp2(t_tile - lse_in[4 + j, side, T:T + 1, :])
                    )
                    weight[rows, cols] = (value * share(j)).astype(jnp.bfloat16)
                    return carry

                lax.fori_loop(0, 4, chunk, 0)

    def part_a_copy(a):
        piece = part_a.at[core, a, other]
        return remote(piece, piece, pa_send.at[a], pa_recv.at[a], sibling)

    def part_b_copy(j):
        piece = part_b.at[core, j, other]
        return remote(piece, piece, pb_send.at[j], pb_recv.at[j], sibling)

    def part_a_arrival(a):
        piece = part_a.at[other, a, core]
        return remote(piece, piece, pa_send.at[a], pa_recv.at[a], sibling)

    def part_b_arrival(j):
        piece = part_b.at[other, j, core]
        return remote(piece, piece, pb_send.at[j], pb_recv.at[j], sibling)

    for a in range(4):
        weights(a)
        term = jnp.dot(
            weight[pl.ds(a * 256, 256), :],
            s_rows[pl.ds(pl.multiple_of(col_base * 256, 256), COLS * 256), :],
            preferred_element_type=jnp.float32,
        ).astype(jnp.bfloat16)
        part_a[core, a] = term.reshape(2, 128, 1024)
        part_a_copy(a).start()

    def slot_base(slot):
        terms = []
        if slot < 4:
            terms += [part_a.at[0, slot, core], part_a.at[1, slot, core]]
        if slot >= 3:
            terms.append(part_b.at[(slot - 3) // 5, (slot - 3) % 5, core])
        return terms

    def slot_wait(slot):
        if slot < 4:
            part_a_arrival(slot).wait_recv()
        if slot >= 3:
            @pl.when(core != (slot - 3) // 5)
            def _():
                part_b_arrival((slot - 3) % 5).wait_recv()

    def sum_copy(slot, src):
        return remote(
            src, stage.at[slot], r_send.at[slot], r_recv.at[slot],
            device(step(PLACE[slot], PLACE[INTO[slot]]), core),
        )

    def slot_terms(slot):
        slot_wait(slot)
        terms = slot_base(slot)
        for child in range(SLOTS):
            if INTO[child] == slot:
                sum_copy(child, stage.at[child]).wait_recv()
                terms.append(stage.at[child])
        return terms

    def send_sum(slot):
        terms = slot_terms(slot)
        if len(terms) == 1:
            sum_copy(slot, terms[0]).start()
        else:
            joined[slot] = functools.reduce(
                lambda p, q: p + q, [term[...].astype(jnp.float32) for term in terms]
            ).astype(jnp.bfloat16)
            sum_copy(slot, joined.at[slot]).start()

    def columns(j):
        term = lax.dot_general(
            weight[:, pl.ds(j * 256, 256)], s_rows[pl.ds(0, 1024), :],
            (((0,), (0,)), ((), ())), preferred_element_type=jnp.float32,
        ).astype(jnp.bfloat16)
        part_b[core, j] = term.reshape(2, 128, 1024)
        part_b_copy(j).start()

    send_sum(0)
    columns(4)
    send_sum(1)
    send_sum(2)
    columns(3)
    send_sum(7)
    send_sum(12)
    columns(2)
    send_sum(6)
    columns(1)
    send_sum(5)
    columns(0)
    send_sum(10)
    for slot in (4, 9, 11, 3):
        send_sum(slot)

    terms = slot_terms(OWN)
    grad = logit_scale * functools.reduce(
        lambda p, q: p + q, [term[...].astype(jnp.float32) for term in terms]
    )
    student = unit[...]
    along = jnp.sum(student * grad, axis=1, keepdims=True)
    d_student = ((grad - student * along) / norm[:, 0:1]).astype(jnp.bfloat16)
    out[...] = lax.dot_general(d_student, proj[...], pair_dims, preferred_element_type=jnp.float32)

    for kind in (T, S):
        for slot in range(SLOTS):
            if slot != OWN:
                row_copy(kind, OWN, slot).wait_send()
            if slot < 4:
                side_copy(kind, slot, half).wait_send()
            else:
                @pl.when(core == (1 if slot < OWN else 0))
                def _(kind=kind, slot=slot):
                    side_copy(kind, slot, half).wait_send()
    for index in range(9):
        for to_half in (0, 1):
            unless_own(index, to_half, lambda: stat_copy(index, to_half).wait_send())
        for of_core in (0, 1):
            if index == 4 and of_core == 1:
                pl.when(core == 0)(lambda: lse_copy(1, 4).wait_send())
            else:
                lse_copy(of_core, index).wait_send()
    for a in range(4):
        part_a_copy(a).wait_send()
    for j in range(COLS):
        part_b_copy(j).wait_send()
    for slot in range(SLOTS):
        if slot != OWN:
            sum_copy(slot, joined.at[slot]).wait_send()


def per_device(features, teacher, proj):
    bf16, f32 = jnp.bfloat16, jnp.float32
    vmem = pl.BlockSpec(memory_space=pltpu.VMEM)
    dma = pltpu.SemaphoreType.DMA
    return pl.pallas_call(
        kernel,
        out_shape=jax.ShapeDtypeStruct((128, 1024), f32),
        in_specs=[vmem] * 3,
        out_specs=vmem,
        scratch_shapes=[
            pltpu.VMEM((SLOTS * 256, 1024), bf16),
            pltpu.VMEM((SLOTS * 256, 1024), bf16),
            pltpu.VMEM((1024, COLS * 256), f32),
            pltpu.VMEM((1024, COLS * 256), f32),
            pltpu.VMEM((1024, COLS * 256), bf16),
            pltpu.VMEM((2, 1024, 128), f32),
            pltpu.VMEM((2, 1024, 128), f32),
            pltpu.VMEM((2, 8, COLS * 256), f32),
            pltpu.VMEM((2, 8, COLS * 256), f32),
            pltpu.VMEM((9, 2, 8, 128), f32),
            pltpu.VMEM((18, 8, 128), f32),
            pltpu.VMEM((8, 128), f32),
            pltpu.VMEM((9, 2, 8, 128), f32),
            pltpu.VMEM((2, 1024, 128), f32),
            pltpu.VMEM((2, 4, 2, 128, 1024), bf16),
            pltpu.VMEM((2, COLS, 2, 128, 1024), bf16),
            pltpu.VMEM((SLOTS, 128, 1024), bf16),
            pltpu.VMEM((SLOTS, 128, 1024), bf16),
            pltpu.VMEM((128, 1024), f32),
            pltpu.VMEM((128, 128), f32),
            dma((2, SLOTS)), dma((2, SLOTS)), dma((2, SLOTS)), dma((2, SLOTS)),
            dma((18,)), dma((18,)), dma((18,)), dma((18,)),
            dma((4,)), dma((4,)), dma((COLS,)), dma((COLS,)), dma((SLOTS,)), dma((SLOTS,)),
        ],
        compiler_params=pltpu.CompilerParams(
            collective_id=0, has_side_effects=True, vmem_limit_bytes=60 * 2**20
        ),
        cost_estimate=pl.CostEstimate(flops=9_000_000_000, bytes_accessed=4_000_000, transcendentals=9_000_000),
    )(features, teacher, proj)


def solution(mesh):
    in_specs = (P(("sub", "dp", "mp"), None), P(("sub", "dp", "mp"), None), P())
    out_specs = P(("sub", "dp", "mp"), None)
    return jax.shard_map(
        per_device, mesh=mesh, in_specs=in_specs, out_specs=out_specs, check_vma=False
    )
```

```python
import functools

import jax
import jax.numpy as jnp
from jax import lax
from jax.experimental import pallas as pl
from jax.experimental.pallas import tpu as pltpu
from jax.sharding import PartitionSpec as P

MESH = pl.DeviceIdType.MESH
logit_scale = 100.0
epsilon = 1e-06
log2e = 1.4426950408889634
NEG = -1e30

PLACE = (
    (2, 3, 0), (1, 3, 0), (3, 3, 0), (0, 3, 0), (0, 0, 3), (0, 3, 1), (0, 1, 3), (0, 3, 2),
    (0, 0, 0), (0, 0, 1), (0, 1, 0), (0, 0, 2), (0, 1, 2),
)
SLOTS = 13
OWN = 8
COLS = 5
SHARE = ((0.5, 1.0, 1.0, 1.0, 0.5), (1.0, 1.0, 0.5, 1.0, 0.5))
FROM = (
    ((1, 3, 3, 8, 8, 3, 4, 11, -1, 8, 8, 9, 6), (2, 3, 3, 8, 8, 9, 4, 5, -1, 8, 8, 9, 11)),
    ((1, 3, 3, 8, 8, 9, 4, 5, -1, 8, 8, 4, 11), (2, 3, 3, 8, 8, 9, 10, 11, -1, 8, 8, 4, 6)),
)
INTO = (
    ((1, 3, 3, 8, 8, 9, 10, 11, -1, 8, 8, 8, 11), (2, 3, 3, 8, 8, 9, 10, 11, -1, 8, 8, 8, 11)),
    ((1, 3, 3, 8, 8, 3, 4, 11, -1, 8, 8, 8, 11), (2, 3, 3, 8, 8, 3, 4, 11, -1, 8, 8, 8, 11)),
)
T, S = 0, 1


def step(a, b):
    return tuple((p - q) % 4 for p, q in zip(a, b))


NEIGHBOURS = ((1, 0, 0), (3, 0, 0), (0, 1, 0), (0, 3, 0), (0, 0, 1), (0, 0, 3))


def rows_of(slot, count=1):
    return pl.ds(slot * 256, count * 256)


def kernel(
    features, teacher, proj, out,
    s_rows, t_rows, s_score, t_score, weight, top_parts, sum_parts, col_top, col_sum,
    stat_out, stat_in, lse_out, lse_in, lse_rows, part_a, part_b, stage, joined,
    unit, norm,
    g_send, g_recv, c_send, c_recv, st_send, st_recv, l_send, l_recv,
    pa_send, pa_recv, pb_send, pb_recv, r_send, r_recv,
):
    sub, dp, mp = lax.axis_index("sub"), lax.axis_index("dp"), lax.axis_index("mp")
    x, y, z, core = sub * 2 + mp // 2, dp % 4, dp // 4, mp % 2
    other = 1 - core
    half = core * 128
    sibling = (sub, dp, (mp // 2) * 2 + other)
    rows_buf = (t_rows, s_rows)
    score_buf = (t_score, s_score)

    def device(move, to_core):
        ax, ay, az = (x + move[0]) % 4, (y + move[1]) % 4, (z + move[2]) % 4
        return (ax // 2, az * 4 + ay, (ax % 2) * 2 + to_core)

    barrier = pltpu.get_barrier_semaphore()
    for move in NEIGHBOURS:
        pl.semaphore_signal(barrier, inc=1, device_id=device(move, core), device_id_type=MESH)
    pl.semaphore_signal(barrier, inc=1, device_id=sibling, device_id_type=MESH)

    def remote(src, dst, send, recv, target):
        return pltpu.make_async_remote_copy(
            src_ref=src, dst_ref=dst, send_sem=send, recv_sem=recv, device_id=target, device_id_type=MESH
        )

    def half_rows(kind, slot, which):
        return rows_buf[kind].at[pl.ds(slot * 256 + which, 128)]

    def row_copy(kind, src_slot, slot):
        move = step(PLACE[src_slot], PLACE[slot])
        return remote(
            half_rows(kind, src_slot, half), half_rows(kind, slot, half),
            g_send.at[kind, slot], g_recv.at[kind, slot], device(move, core),
        )

    def side_copy(kind, slot, which):
        piece = half_rows(kind, slot, which)
        return remote(piece, piece, c_send.at[kind, slot], c_recv.at[kind, slot], sibling)

    def to_side(kind, slot):
        if slot < 4:
            side_copy(kind, slot, half).start()
        else:
            @pl.when(core == (1 if slot < OWN else 0))
            def _():
                side_copy(kind, slot, half).start()

    def forward(kind, slot):
        for which in (0, 1):
            children = [d for d in range(SLOTS) if FROM[kind][which][d] == slot]
            if children:
                @pl.when(core == which)
                def _(children=children):
                    for child in children:
                        row_copy(kind, slot, child).start()
        to_side(kind, slot)

    def arrive(kind, slot):
        row_copy(kind, OWN, slot).wait_recv()
        forward(kind, slot)

    def side_wait(kind, *slots):
        for slot in slots:
            if slot < 4:
                side_copy(kind, slot, 128 - half).wait_recv()
            else:
                @pl.when(core == (0 if slot < OWN else 1))
                def _(slot=slot):
                    side_copy(kind, slot, 128 - half).wait_recv()

    own_rows = pl.ds(OWN * 256 + half, 128)
    values = teacher[...].astype(jnp.float32)
    t_rows[own_rows, :] = (
        values / jnp.sqrt(jnp.sum(values * values, axis=1, keepdims=True) + epsilon)
    ).astype(jnp.bfloat16)

    pl.semaphore_wait(barrier, len(NEIGHBOURS) + 1)
    forward(T, OWN)

    student = jnp.dot(features[...], proj[...], preferred_element_type=jnp.float32)
    length = jnp.sqrt(jnp.sum(student * student, axis=1, keepdims=True) + epsilon)
    student = student / length
    unit[...] = student
    norm[...] = jnp.broadcast_to(length, norm.shape)
    s_rows[own_rows, :] = student.astype(jnp.bfloat16)
    forward(S, OWN)

    for kind in (T, S):
        top_parts[kind] = jnp.full(top_parts.shape[1:], NEG, jnp.float32)
        sum_parts[kind] = jnp.zeros(sum_parts.shape[1:], jnp.float32)
        col_top[kind] = jnp.full(col_top.shape[1:], NEG, jnp.float32)
        col_sum[kind] = jnp.zeros(col_sum.shape[1:], jnp.float32)

    col_base = 3 + COLS * core
    pair_dims = (((1,), (1,)), ((), ()))
    lanes = lax.broadcasted_iota(jnp.int32, (256, 128), 1)

    def scores(kind, a0, na, j0, nj):
        buf, score = rows_buf[kind], score_buf[kind]

        def column(i, carry):
            j = j0 + i
            cols = buf[pl.ds(pl.multiple_of((col_base + j) * 256, 256), 256), :]
            score[pl.ds(a0 * 256, na * 256), pl.ds(pl.multiple_of(j * 256, 256), 256)] = (
                lax.dot_general(
                    buf[pl.ds(a0 * 256, na * 256), :], cols, pair_dims, preferred_element_type=jnp.float32
                ) * (logit_scale * log2e)
            )
            return carry

        lax.fori_loop(0, nj, column, 0)
        if a0 <= 3 < a0 + na and j0 == 0:
            @pl.when(core == 0)
            def _():
                tile = score[pl.ds(768, 256), pl.ds(0, 256)]
                row = lax.broadcasted_iota(jnp.int32, (256, 256), 0)
                col = lax.broadcasted_iota(jnp.int32, (256, 256), 1)
                score[pl.ds(768, 256), pl.ds(0, 256)] = jnp.where(row == col, NEG, tile)

        def totals(i, carry):
            a, j = a0 + i // nj, j0 + i % nj
            rows = pl.ds(pl.multiple_of(a * 256, 256), 256)
            cols = pl.ds(pl.multiple_of(j * 256, 256), 256)
            tile = score[rows, cols]
            top = jnp.max(tile, axis=1, keepdims=True)
            total = jnp.sum(jnp.exp2(tile - top), axis=1, keepdims=True)
            here = lanes == j
            top_parts[kind, rows, :] = jnp.where(here, top, top_parts[kind, rows, :])
            sum_parts[kind, rows, :] = jnp.where(here, total, sum_parts[kind, rows, :])
            top = jnp.max(tile, axis=0, keepdims=True)
            total = jnp.sum(jnp.exp2(tile - top), axis=0, keepdims=True)
            col_top[kind, pl.ds(a, 1), cols] = top
            col_sum[kind, pl.ds(a, 1), cols] = total
            return carry

        lax.fori_loop(0, na * nj, totals, 0)

    for kind, slot in ((T, 3), (T, 9), (T, 4), (T, 10), (S, 3), (S, 9), (S, 4), (S, 10)):
        arrive(kind, slot)
    for kind, slot in ((T, 1), (T, 2), (S, 1), (S, 2)):
        arrive(kind, slot)
    for kind in (T, S):
        side_wait(kind, 3, 4, 8, 9)
        scores(kind, 3, 1, 0, 2)
    for kind, slot in ((T, 6), (T, 11), (T, 5), (S, 6), (S, 11), (S, 5)):
        arrive(kind, slot)
    for kind in (T, S):
        side_wait(kind, 1, 2)
        scores(kind, 1, 2, 0, 2)
    for kind, slot in ((T, 0), (S, 0)):
        arrive(kind, slot)
    for kind in (T, S):
        side_wait(kind, 5, 6, 10, 11)
        scores(kind, 1, 3, 2, 2)
    for kind, slot in ((T, 7), (T, 12), (S, 7), (S, 12)):
        arrive(kind, slot)
    for kind in (T, S):
        side_wait(kind, 0)
        scores(kind, 0, 1, 0, 4)
    for kind in (T, S):
        side_wait(kind, 7, 12)
        scores(kind, 0, 4, 4, 1)

    def share(j):
        return jnp.where(core == 0, SHARE[0][j], SHARE[1][j]).astype(jnp.float32)

    shares = [share(j) for j in range(COLS)]
    share_lanes = jnp.zeros((256, 128), jnp.float32)
    for j in range(COLS):
        share_lanes = jnp.where(lanes == j, share(j), share_lanes)

    for a in range(4):
        rows = pl.ds(a * 256, 256)
        packed = jnp.zeros((256, 128), jnp.float32)
        for kind in (T, S):
            parts = top_parts[kind, rows, :]
            top = jnp.max(parts, axis=1, keepdims=True)
            total = jnp.sum(
                sum_parts[kind, rows, :] * share_lanes * jnp.exp2(parts - top), axis=1, keepdims=True
            )
            packed = jnp.where(lanes == 2 * kind, top, packed)
            packed = jnp.where(lanes == 2 * kind + 1, total, packed)
        turned = packed.T
        stat_out[a, 0] = turned[0:8, 0:128]
        stat_out[a, 1] = turned[0:8, 128:256]
    for j in range(COLS):
        cols = pl.ds(j * 256, 256)
        lines = []
        for kind in (T, S):
            parts = col_top[kind, :, cols]
            top = jnp.max(parts, axis=0, keepdims=True)
            total = jnp.sum(col_sum[kind, :, cols] * jnp.exp2(parts - top), axis=0, keepdims=True)
            lines += [top, total * share(j)]
        lines.append(jnp.zeros((4, 256), jnp.float32))
        lines = jnp.concatenate(lines, axis=0)
        stat_out[4 + j, 0] = lines[:, 0:128]
        stat_out[4 + j, 1] = lines[:, 128:256]

    def place_at(index, of_core):
        if index < 4:
            return PLACE[index]
        first, second = PLACE[index - 1], PLACE[index + 4]
        return tuple(jnp.where(of_core == 0, p, q) for p, q in zip(first, second))

    def back(move):
        return tuple(4 - m for m in move)

    def stat_copy(index, to_half):
        return remote(
            stat_out.at[index, to_half], stat_in.at[core * 9 + index],
            st_send.at[index * 2 + to_half], st_recv.at[core * 9 + index],
            device(place_at(index, core), to_half),
        )

    def unless_own(index, to_half, action, instead=None):
        if index == 4 and to_half == 1:
            pl.when(core == 0)(action)
            if instead is not None:
                pl.when(core == 1)(instead)
        else:
            action()

    def keep_stat():
        stat_in[9 + 4] = stat_out[4, 1]

    for index in range(9):
        for to_half in (0, 1):
            unless_own(index, to_half, lambda: stat_copy(index, to_half).start(), keep_stat)

    def stat_arrival(source):
        return remote(
            stat_out.at[0, 0], stat_in.at[source], st_send.at[0], st_recv.at[source], sibling
        )

    for source in range(18):
        if source == 9 + 4:
            pl.when(core == 0)(lambda: stat_arrival(13).wait_recv())
        else:
            stat_arrival(source).wait_recv()

    lines = []
    for kind in (T, S):
        tops = stat_in[:, 2 * kind, :]
        top = jnp.max(tops, axis=0, keepdims=True)
        total = jnp.sum(stat_in[:, 2 * kind + 1, :] * jnp.exp2(tops - top), axis=0, keepdims=True)
        lines.append(top + jnp.log(total) * log2e)
    lines.append(jnp.zeros((6, 128), jnp.float32))
    lse_out[...] = jnp.concatenate(lines, axis=0)

    def lse_copy(of_core, index):
        return remote(
            lse_out, lse_in.at[index, core],
            l_send.at[of_core * 9 + index], l_recv.at[index * 2 + core],
            device(back(place_at(index, jnp.int32(of_core)) if index < 4 else PLACE[index - 1 + 5 * of_core]), of_core),
        )

    def lse_arrival(index, from_half):
        return remote(
            lse_out, lse_in.at[index, from_half], l_send.at[0], l_recv.at[index * 2 + from_half], sibling
        )

    def keep_lse():
        lse_in[4, 1] = lse_out[...]

    for index in range(9):
        for of_core in (0, 1):
            if index == 4 and of_core == 1:
                pl.when(core == 0)(lambda: lse_copy(1, 4).start())
                pl.when(core == 1)(keep_lse)
            else:
                lse_copy(of_core, index).start()
    for index in range(9):
        for from_half in (0, 1):
            unless_own(index, from_half, lambda: lse_arrival(index, from_half).wait_recv())

    for a in range(4):
        lines = jnp.concatenate(
            [
                jnp.concatenate([lse_in[a, 0], lse_in[a, 1]], axis=1),
                jnp.zeros((120, 256), jnp.float32),
            ],
            axis=0,
        ).T
        for kind in (T, S):
            lse_rows[kind, pl.ds(a * 256, 256), :] = jnp.broadcast_to(lines[:, kind:kind + 1], (256, 128))

    def weights(a):
        for j in range(COLS):
            for side in (0, 1):
                for i in range(4):
                    rows = pl.ds(a * 256 + i * 64, 64)
                    cols = pl.ds(j * 256 + side * 128, 128)
                    s_tile, t_tile = s_score[rows, cols], t_score[rows, cols]
                    value = (
                        jnp.exp2(s_tile - lse_rows[S, rows, :])
                        + jnp.exp2(s_tile - lse_in[4 + j, side, S:S + 1, :])
                        - jnp.exp2(t_tile - lse_rows[T, rows, :])
                        - jnp.exp2(t_tile - lse_in[4 + j, side, T:T + 1, :])
                    )
                    weight[rows, cols] = (value * shares[j]).astype(jnp.bfloat16)

    def part_a_copy(a):
        piece = part_a.at[core, a, other]
        return remote(piece, piece, pa_send.at[a], pa_recv.at[a], sibling)

    def part_b_copy(j):
        piece = part_b.at[core, j, other]
        return remote(piece, piece, pb_send.at[j], pb_recv.at[j], sibling)

    def part_a_arrival(a):
        piece = part_a.at[other, a, core]
        return remote(piece, piece, pa_send.at[a], pa_recv.at[a], sibling)

    def part_b_arrival(j):
        piece = part_b.at[other, j, core]
        return remote(piece, piece, pb_send.at[j], pb_recv.at[j], sibling)

    def rows_term(a):
        term = jnp.dot(
            weight[pl.ds(a * 256, 256), :],
            s_rows[pl.ds(pl.multiple_of(col_base * 256, 256), COLS * 256), :],
            preferred_element_type=jnp.float32,
        ).astype(jnp.bfloat16)
        part_a[core, a] = term.reshape(2, 128, 1024)

    def columns_term(j):
        term = lax.dot_general(
            weight[:, pl.ds(j * 256, 256)], s_rows[pl.ds(0, 1024), :],
            (((0,), (0,)), ((), ())), preferred_element_type=jnp.float32,
        ).astype(jnp.bfloat16)
        part_b[core, j] = term.reshape(2, 128, 1024)
        part_b_copy(j).start()

    def piece_of(ref, piece):
        return ref.at[pl.ds(piece * 64, 64), :]

    def slot_ready(slot):
        if slot < 4:
            part_a_arrival(slot).wait_recv()
        if slot >= 3:
            @pl.when(core != (slot - 3) // 5)
            def _():
                part_b_arrival((slot - 3) % 5).wait_recv()

    def sum_copy(which, slot, piece, src):
        into = INTO[which][piece][slot]
        return remote(
            piece_of(src, piece), piece_of(stage.at[slot], piece),
            r_send.at[slot * 2 + piece], r_recv.at[slot * 2 + piece],
            device(step(PLACE[slot], PLACE[into]), core),
        )

    def slot_terms(which, slot, piece):
        terms = []
        if slot < 4:
            terms += [part_a.at[0, slot, core], part_a.at[1, slot, core]]
        if slot >= 3:
            terms.append(part_b.at[(slot - 3) // 5, (slot - 3) % 5, core])
        for child in range(SLOTS):
            if INTO[which][piece][child] == slot:
                sum_copy(which, child, piece, stage.at[child]).wait_recv()
                terms.append(stage.at[child])
        return terms

    def added(terms, piece):
        return functools.reduce(
            lambda p, q: p + q, [piece_of(term, piece)[...].astype(jnp.float32) for term in terms]
        )

    def send_sum(slot, *pieces):
        def send(which):
            for piece in pieces:
                terms = slot_terms(which, slot, piece)
                if len(terms) == 1:
                    sum_copy(which, slot, piece, terms[0]).start()
                else:
                    piece_of(joined.at[slot], piece)[...] = added(terms, piece).astype(jnp.bfloat16)
                    sum_copy(which, slot, piece, joined.at[slot]).start()

        routes = [
            [(INTO[which][piece][slot], [c for c in range(SLOTS) if INTO[which][piece][c] == slot]) for piece in pieces]
            for which in (0, 1)
        ]
        if routes[0] == routes[1]:
            send(0)
        else:
            pl.when(core == 0)(lambda: send(0))
            pl.when(core == 1)(lambda: send(1))

    weights(0)
    for a in range(4):
        rows_term(a)
        if a < 3:
            weights(a + 1)
        part_a_copy(a).start()
        if a == 2:
            slot_ready(0)
            send_sum(0, 0, 1)
            slot_ready(1)
            send_sum(1, 1)
        if a == 3:
            slot_ready(2)
            send_sum(2, 0)
    columns_term(4)
    columns_term(3)
    for slot in (7, 12):
        slot_ready(slot)
        send_sum(slot, 0, 1)
    send_sum(1, 0)
    send_sum(2, 1)
    columns_term(2)
    for slot in (6, 11):
        slot_ready(slot)
    send_sum(6, 0, 1)
    columns_term(1)
    for slot in (5, 10):
        slot_ready(slot)
    send_sum(5, 0, 1)
    columns_term(0)
    for slot in (4, 9, 3, 8):
        slot_ready(slot)
    for piece in (0, 1):
        for slot in (11, 10, 4, 9, 3):
            send_sum(slot, piece)

    grad = logit_scale * jnp.concatenate(
        [added(slot_terms(0, OWN, piece), piece) for piece in (0, 1)], axis=0
    )
    student = unit[...]
    along = jnp.sum(student * grad, axis=1, keepdims=True)
    d_student = ((grad - student * along) / norm[:, 0:1]).astype(jnp.bfloat16)
    out[...] = lax.dot_general(d_student, proj[...], pair_dims, preferred_element_type=jnp.float32)

    for kind in (T, S):
        for slot in range(SLOTS):
            if slot != OWN:
                row_copy(kind, OWN, slot).wait_send()
            if slot < 4:
                side_copy(kind, slot, half).wait_send()
            else:
                @pl.when(core == (1 if slot < OWN else 0))
                def _(kind=kind, slot=slot):
                    side_copy(kind, slot, half).wait_send()
    for index in range(9):
        for to_half in (0, 1):
            unless_own(index, to_half, lambda: stat_copy(index, to_half).wait_send())
        for of_core in (0, 1):
            if index == 4 and of_core == 1:
                pl.when(core == 0)(lambda: lse_copy(1, 4).wait_send())
            else:
                lse_copy(of_core, index).wait_send()
    for a in range(4):
        part_a_copy(a).wait_send()
    for j in range(COLS):
        part_b_copy(j).wait_send()
    for slot in range(SLOTS):
        if slot != OWN:
            for piece in (0, 1):
                sum_copy(0, slot, piece, joined.at[slot]).wait_send()


def per_device(features, teacher, proj):
    bf16, f32 = jnp.bfloat16, jnp.float32
    vmem = pl.BlockSpec(memory_space=pltpu.VMEM)
    dma = pltpu.SemaphoreType.DMA
    return pl.pallas_call(
        kernel,
        out_shape=jax.ShapeDtypeStruct((128, 1024), f32),
        in_specs=[vmem] * 3,
        out_specs=vmem,
        scratch_shapes=[
            pltpu.VMEM((SLOTS * 256, 1024), bf16),
            pltpu.VMEM((SLOTS * 256, 1024), bf16),
            pltpu.VMEM((1024, COLS * 256), f32),
            pltpu.VMEM((1024, COLS * 256), f32),
            pltpu.VMEM((1024, COLS * 256), bf16),
            pltpu.VMEM((2, 1024, 128), f32),
            pltpu.VMEM((2, 1024, 128), f32),
            pltpu.VMEM((2, 8, COLS * 256), f32),
            pltpu.VMEM((2, 8, COLS * 256), f32),
            pltpu.VMEM((9, 2, 8, 128), f32),
            pltpu.VMEM((18, 8, 128), f32),
            pltpu.VMEM((8, 128), f32),
            pltpu.VMEM((9, 2, 8, 128), f32),
            pltpu.VMEM((2, 1024, 128), f32),
            pltpu.VMEM((2, 4, 2, 128, 1024), bf16),
            pltpu.VMEM((2, COLS, 2, 128, 1024), bf16),
            pltpu.VMEM((SLOTS, 128, 1024), bf16),
            pltpu.VMEM((SLOTS, 128, 1024), bf16),
            pltpu.VMEM((128, 1024), f32),
            pltpu.VMEM((128, 128), f32),
            dma((2, SLOTS)), dma((2, SLOTS)), dma((2, SLOTS)), dma((2, SLOTS)),
            dma((18,)), dma((18,)), dma((18,)), dma((18,)),
            dma((4,)), dma((4,)), dma((COLS,)), dma((COLS,)), dma((2 * SLOTS,)), dma((2 * SLOTS,)),
        ],
        compiler_params=pltpu.CompilerParams(
            collective_id=0, has_side_effects=True, vmem_limit_bytes=60 * 2**20
        ),
        cost_estimate=pl.CostEstimate(flops=9_000_000_000, bytes_accessed=4_000_000, transcendentals=9_000_000),
    )(features, teacher, proj)


def solution(mesh):
    in_specs = (P(("sub", "dp", "mp"), None), P(("sub", "dp", "mp"), None), P())
    out_specs = P(("sub", "dp", "mp"), None)
    return jax.shard_map(
        per_device, mesh=mesh, in_specs=in_specs, out_specs=out_specs, check_vma=False
    )
```

```python
import functools

import jax
import jax.numpy as jnp
from jax import lax
from jax.experimental import pallas as pl
from jax.experimental.pallas import tpu as pltpu
from jax.sharding import PartitionSpec as P

MESH = pl.DeviceIdType.MESH
logit_scale = 100.0
epsilon = 1e-06
log2e = 1.4426950408889634
NEG = -1e30

PLACE = (
    (2, 3, 0), (1, 3, 0), (3, 3, 0), (0, 3, 0), (0, 0, 3), (0, 3, 1), (0, 1, 3), (0, 3, 2),
    (0, 0, 0), (0, 0, 1), (0, 1, 0), (0, 0, 2), (0, 1, 2),
)
SLOTS = 13
OWN = 8
COLS = 5
SHARE = ((0.5, 1.0, 1.0, 1.0, 0.5), (1.0, 1.0, 0.5, 1.0, 0.5))
FROM = (
    ((2, 3, 3, 8, 8, 9, 4, 5, -1, 8, 8, 4, 6), (2, 3, 3, 8, 8, 9, 10, 11, -1, 8, 8, 9, 6)),
    ((2, 3, 3, 8, 8, 9, 10, 11, -1, 8, 8, 9, 11), (2, 3, 3, 8, 8, 3, 4, 5, -1, 8, 8, 9, 11)),
    ((1, 3, 3, 8, 8, 3, 4, 11, -1, 8, 8, 4, 11), (1, 3, 3, 8, 8, 9, 4, 11, -1, 8, 8, 4, 11)),
    ((1, 3, 3, 8, 8, 9, 4, 5, -1, 8, 8, 9, 6), (1, 3, 3, 8, 8, 9, 4, 5, -1, 8, 8, 4, 6)),
)
FIRST = (
    "S3", "V10", "V4", "V9", "S4", "T3", "T4", "T9", "U4", "V3", "S9", "T10", "U3", "S10", "U10", "U9",
)
INTO = (
    ((2, 3, 3, 8, 8, 9, 4, 5, -1, 8, 8, 9, 10), (2, 3, 3, 8, 8, 9, 4, 11, -1, 8, 8, 4, 11)),
    ((1, 3, 3, 8, 8, 9, 4, 5, -1, 8, 8, 9, 10), (1, 3, 3, 8, 8, 9, 4, 11, -1, 8, 8, 4, 6)),
)
ORDER = (
    "W0", "A0", "W1", "W2", "W3", "B4", "0.0", "A1", "7.0", "7.1", "0.1", "12.1", "A2", "B2", "12.0", "B3",
    "5.1", "6.0", "1.0", "2.0", "B1", "A3", "5.0", "1.1", "11.0", "11.1", "6.1", "B0", "2.1", "10.1", "4.0", "9.1", "3.0", "10.0", "9.0", "3.1", "4.1",
)
T, S = 0, 1


def step(a, b):
    return tuple((p - q) % 4 for p, q in zip(a, b))


NEIGHBOURS = ((1, 0, 0), (3, 0, 0), (0, 1, 0), (0, 3, 0), (0, 0, 1), (0, 0, 3))


def rows_of(slot, count=1):
    return pl.ds(slot * 256, count * 256)


def kernel(
    features_in, teacher_in, proj_in, out,
    features, teacher, proj,
    s_rows, t_rows, s_score, t_score, weight, top_parts, sum_parts, col_top, col_sum,
    stat_out, stat_in, lse_out, lse_in, lse_rows, part_a, part_b, stage, joined,
    unit, norm,
    g_send, g_recv, c_send, c_recv, st_send, st_recv, l_send, l_recv,
    pa_send, pa_recv, pb_send, pb_recv, r_send, r_recv, in_sem,
):
    loads = [
        pltpu.make_async_copy(src, dst, in_sem.at[i])
        for i, (src, dst) in enumerate(((teacher_in, teacher), (features_in, features), (proj_in, proj)))
    ]
    for load in loads:
        load.start()

    sub, dp, mp = lax.axis_index("sub"), lax.axis_index("dp"), lax.axis_index("mp")
    x, y, z, core = sub * 2 + mp // 2, dp % 4, dp // 4, mp % 2
    other = 1 - core
    half = core * 128
    sibling = (sub, dp, (mp // 2) * 2 + other)
    rows_buf = (t_rows, s_rows)
    score_buf = (t_score, s_score)

    def device(move, to_core):
        ax, ay, az = (x + move[0]) % 4, (y + move[1]) % 4, (z + move[2]) % 4
        return (ax // 2, az * 4 + ay, (ax % 2) * 2 + to_core)

    barrier = pltpu.get_barrier_semaphore()
    for move in NEIGHBOURS:
        pl.semaphore_signal(barrier, inc=1, device_id=device(move, core), device_id_type=MESH)
    pl.semaphore_signal(barrier, inc=1, device_id=sibling, device_id_type=MESH)

    def remote(src, dst, send, recv, target):
        return pltpu.make_async_remote_copy(
            src_ref=src, dst_ref=dst, send_sem=send, recv_sem=recv, device_id=target, device_id_type=MESH
        )

    def piece_rows(q, slot, which):
        return rows_buf[q // 2].at[pl.ds(slot * 256 + which + (q % 2) * 64, 64)]

    def row_copy(q, src_slot, slot):
        move = step(PLACE[src_slot], PLACE[slot])
        return remote(
            piece_rows(q, src_slot, half), piece_rows(q, slot, half),
            g_send.at[q, slot], g_recv.at[q, slot], device(move, core),
        )

    def side_copy(q, slot, which):
        piece = piece_rows(q, slot, which)
        return remote(piece, piece, c_send.at[q, slot], c_recv.at[q, slot], sibling)

    def to_side(q, slot):
        if slot < 4:
            side_copy(q, slot, half).start()
        else:
            @pl.when(core == (1 if slot < OWN else 0))
            def _():
                side_copy(q, slot, half).start()

    def start_rows(q, slot, children):
        for child in children:
            row_copy(q, slot, child).start()

    def arrive(q, slot):
        row_copy(q, OWN, slot).wait_recv()
        children = [[d for d in range(SLOTS) if FROM[q][which][d] == slot] for which in (0, 1)]
        if children[0] == children[1]:
            start_rows(q, slot, children[0])
        else:
            for which in (0, 1):
                if children[which]:
                    pl.when(core == which)(lambda: start_rows(q, slot, children[which]))
        to_side(q, slot)

    def side_wait(kind, *slots):
        for slot in slots:
            for q in (2 * kind, 2 * kind + 1):
                if slot < 4:
                    side_copy(q, slot, 128 - half).wait_recv()
                else:
                    @pl.when(core == (0 if slot < OWN else 1))
                    def _(slot=slot, q=q):
                        side_copy(q, slot, 128 - half).wait_recv()

    own_rows = pl.ds(OWN * 256 + half, 128)
    loads[0].wait()
    values = teacher[...].astype(jnp.float32)
    t_rows[own_rows, :] = (
        values / jnp.sqrt(jnp.sum(values * values, axis=1, keepdims=True) + epsilon)
    ).astype(jnp.bfloat16)
    loads[1].wait()
    loads[2].wait()
    student = jnp.dot(features[...], proj[...], preferred_element_type=jnp.float32)
    length = jnp.sqrt(jnp.sum(student * student, axis=1, keepdims=True) + epsilon)
    student = student / length
    unit[...] = student
    norm[...] = jnp.broadcast_to(length, norm.shape)
    s_rows[own_rows, :] = student.astype(jnp.bfloat16)

    pl.semaphore_wait(barrier, len(NEIGHBOURS) + 1)
    for name in FIRST:
        start_rows("TUSV".index(name[0]), OWN, (int(name[1:]),))
    for q in range(4):
        to_side(q, OWN)

    for kind in (T, S):
        top_parts[kind] = jnp.full(top_parts.shape[1:], NEG, jnp.float32)
        sum_parts[kind] = jnp.zeros(sum_parts.shape[1:], jnp.float32)
        col_top[kind] = jnp.full(col_top.shape[1:], NEG, jnp.float32)
        col_sum[kind] = jnp.zeros(col_sum.shape[1:], jnp.float32)

    col_base = 3 + COLS * core
    pair_dims = (((1,), (1,)), ((), ()))
    lanes = lax.broadcasted_iota(jnp.int32, (256, 128), 1)

    def share(j):
        return jnp.where(core == 0, SHARE[0][j], SHARE[1][j]).astype(jnp.float32)

    shares = [share(j) for j in range(COLS)]

    def scores(*pieces):
        def product(kind, a0, na, j):
            buf = rows_buf[kind]
            score_buf[kind][pl.ds(a0 * 256, na * 256), pl.ds(j * 256, 256)] = lax.dot_general(
                buf[pl.ds(a0 * 256, na * 256), :],
                buf[pl.ds(pl.multiple_of((col_base + j) * 256, 256), 256), :],
                pair_dims, preferred_element_type=jnp.float32,
            ) * (logit_scale * log2e)
            if a0 <= 3 < a0 + na and j == 0:
                @pl.when(core == 0)
                def _():
                    tile = score_buf[kind][pl.ds(768, 256), pl.ds(0, 256)]
                    row = lax.broadcasted_iota(jnp.int32, (256, 256), 0)
                    col = lax.broadcasted_iota(jnp.int32, (256, 256), 1)
                    score_buf[kind][pl.ds(768, 256), pl.ds(0, 256)] = jnp.where(row == col, NEG, tile)

        def totals(kind, a0, na, j):
            cols = pl.ds(j * 256, 256)
            for a in range(a0, a0 + na):
                for i in range(4):
                    rows = pl.ds(a * 256 + i * 64, 64)
                    first = score_buf[kind][rows, pl.ds(j * 256, 128)]
                    second = score_buf[kind][rows, pl.ds(j * 256 + 128, 128)]
                    before = top_parts[kind, rows, :]
                    top = jnp.maximum(before, jnp.maximum(first, second))
                    total = jnp.exp2(first - top) + jnp.exp2(second - top)
                    sum_parts[kind, rows, :] = sum_parts[kind, rows, :] * jnp.exp2(before - top) + total * shares[j]
                    top_parts[kind, rows, :] = top
                tile = score_buf[kind][pl.ds(a * 256, 256), cols]
                top = jnp.max(tile, axis=0, keepdims=True)
                total = jnp.sum(jnp.exp2(tile - top), axis=0, keepdims=True)
                col_top[kind, a:a + 1, cols] = top
                col_sum[kind, a:a + 1, cols] = total

        product(*pieces[0])
        for last, piece in zip(pieces, pieces[1:]):
            totals(*last)
            product(*piece)
        totals(*pieces[-1])

    def arrivals(*names):
        for name in names:
            arrive("TUSV".index(name[0]), int(name[1:]))

    arrivals("S3", "V4", "V10", "V9", "T3", "T10", "S4", "T9", "S1", "S2", "V3", "S10", "T4", "S9", "T1", "T2", "U3", "U10", "U4", "U9", "V1", "V2")
    side_wait(S, 1, 2, 3, 4, 8, 9)
    scores((S, 1, 3, 0), (S, 1, 3, 1))
    arrivals("V5", "V6", "S0", "U2", "T5", "S6", "S11", "V11", "T11")
    side_wait(S, 6, 11)
    scores((S, 1, 3, 3))
    arrivals("U1", "T0", "S5", "U5", "T6", "U6", "U11")
    side_wait(T, 1, 2, 3, 4, 8, 9)
    side_wait(S, 5, 10)
    scores((T, 1, 3, 0), (T, 1, 3, 1), (S, 1, 3, 2))
    arrivals("V0", "U0", "S7", "S12", "V12", "V7")
    side_wait(T, 5, 6, 10, 11)
    side_wait(S, 0)
    scores((T, 1, 3, 2), (T, 1, 3, 3), *((S, 0, 1, j) for j in range(4)))
    arrivals("T12", "U12", "T7", "U7")
    side_wait(T, 0)
    side_wait(S, 7, 12)
    scores(*((T, 0, 1, j) for j in range(4)), (S, 0, 4, 4))
    side_wait(T, 7, 12)
    scores((T, 0, 4, 4))

    for a in range(4):
        rows = pl.ds(a * 256, 256)
        packed = jnp.zeros((256, 128), jnp.float32)
        for kind in (T, S):
            parts = top_parts[kind, rows, :]
            top = jnp.max(parts, axis=1, keepdims=True)
            total = jnp.sum(sum_parts[kind, rows, :] * jnp.exp2(parts - top), axis=1, keepdims=True)
            packed = jnp.where(lanes == 2 * kind, top, packed)
            packed = jnp.where(lanes == 2 * kind + 1, total, packed)
        turned = packed.T
        stat_out[a, 0] = turned[0:8, 0:128]
        stat_out[a, 1] = turned[0:8, 128:256]
    for j in range(COLS):
        cols = pl.ds(j * 256, 256)
        lines = []
        for kind in (T, S):
            parts = col_top[kind, :, cols]
            top = jnp.max(parts, axis=0, keepdims=True)
            total = jnp.sum(col_sum[kind, :, cols] * jnp.exp2(parts - top), axis=0, keepdims=True)
            lines += [top, total * shares[j]]
        lines.append(jnp.zeros((4, 256), jnp.float32))
        lines = jnp.concatenate(lines, axis=0)
        stat_out[4 + j, 0] = lines[:, 0:128]
        stat_out[4 + j, 1] = lines[:, 128:256]

    def place_at(index, of_core):
        if index < 4:
            return PLACE[index]
        first, second = PLACE[index - 1], PLACE[index + 4]
        return tuple(jnp.where(of_core == 0, p, q) for p, q in zip(first, second))

    def back(move):
        return tuple(4 - m for m in move)

    def stat_copy(index, to_half):
        return remote(
            stat_out.at[index, to_half], stat_in.at[core * 9 + index],
            st_send.at[index * 2 + to_half], st_recv.at[core * 9 + index],
            device(place_at(index, core), to_half),
        )

    def unless_own(index, to_half, action, instead=None):
        if index == 4 and to_half == 1:
            pl.when(core == 0)(action)
            if instead is not None:
                pl.when(core == 1)(instead)
        else:
            action()

    def keep_stat():
        stat_in[9 + 4] = stat_out[4, 1]

    for index in range(9):
        for to_half in (0, 1):
            unless_own(index, to_half, lambda: stat_copy(index, to_half).start(), keep_stat)

    def stat_arrival(source):
        return remote(
            stat_out.at[0, 0], stat_in.at[source], st_send.at[0], st_recv.at[source], sibling
        )

    for source in range(18):
        if source == 9 + 4:
            pl.when(core == 0)(lambda: stat_arrival(13).wait_recv())
        else:
            stat_arrival(source).wait_recv()

    lines = []
    for kind in (T, S):
        tops = stat_in[:, 2 * kind, :]
        top = jnp.max(tops, axis=0, keepdims=True)
        total = jnp.sum(stat_in[:, 2 * kind + 1, :] * jnp.exp2(tops - top), axis=0, keepdims=True)
        lines.append(top + jnp.log(total) * log2e)
    lines.append(jnp.zeros((6, 128), jnp.float32))
    lse_out[...] = jnp.concatenate(lines, axis=0)

    def lse_copy(of_core, index):
        return remote(
            lse_out, lse_in.at[index, core],
            l_send.at[of_core * 9 + index], l_recv.at[index * 2 + core],
            device(back(place_at(index, jnp.int32(of_core)) if index < 4 else PLACE[index - 1 + 5 * of_core]), of_core),
        )

    def lse_arrival(index, from_half):
        return remote(
            lse_out, lse_in.at[index, from_half], l_send.at[0], l_recv.at[index * 2 + from_half], sibling
        )

    def keep_lse():
        lse_in[4, 1] = lse_out[...]

    for index in range(9):
        for of_core in (0, 1):
            if index == 4 and of_core == 1:
                pl.when(core == 0)(lambda: lse_copy(1, 4).start())
                pl.when(core == 1)(keep_lse)
            else:
                lse_copy(of_core, index).start()
    for index in range(9):
        for from_half in (0, 1):
            unless_own(index, from_half, lambda: lse_arrival(index, from_half).wait_recv())

    for a in range(4):
        lines = jnp.concatenate(
            [
                jnp.concatenate([lse_in[a, 0], lse_in[a, 1]], axis=1),
                jnp.zeros((120, 256), jnp.float32),
            ],
            axis=0,
        ).T
        for kind in (T, S):
            lse_rows[kind, pl.ds(a * 256, 256), :] = jnp.broadcast_to(lines[:, kind:kind + 1], (256, 128))

    def weights(a):
        for j in range(COLS):
            for side in (0, 1):
                for i in range(4):
                    rows = pl.ds(a * 256 + i * 64, 64)
                    cols = pl.ds(j * 256 + side * 128, 128)
                    s_tile, t_tile = s_score[rows, cols], t_score[rows, cols]
                    value = (
                        jnp.exp2(s_tile - lse_rows[S, rows, :])
                        + jnp.exp2(s_tile - lse_in[4 + j, side, S:S + 1, :])
                        - jnp.exp2(t_tile - lse_rows[T, rows, :])
                        - jnp.exp2(t_tile - lse_in[4 + j, side, T:T + 1, :])
                    )
                    weight[rows, cols] = (value * shares[j]).astype(jnp.bfloat16)

    def part_a_copy(a):
        piece = part_a.at[core, a, other]
        return remote(piece, piece, pa_send.at[a], pa_recv.at[a], sibling)

    def part_b_copy(j):
        piece = part_b.at[core, j, other]
        return remote(piece, piece, pb_send.at[j], pb_recv.at[j], sibling)

    def part_a_arrival(a):
        piece = part_a.at[other, a, core]
        return remote(piece, piece, pa_send.at[a], pa_recv.at[a], sibling)

    def part_b_arrival(j):
        piece = part_b.at[other, j, core]
        return remote(piece, piece, pb_send.at[j], pb_recv.at[j], sibling)

    def rows_term(a):
        term = jnp.dot(
            weight[pl.ds(a * 256, 256), :],
            s_rows[pl.ds(pl.multiple_of(col_base * 256, 256), COLS * 256), :],
            preferred_element_type=jnp.float32,
        ).astype(jnp.bfloat16)
        part_a[core, a] = term.reshape(2, 128, 1024)

    def columns_term(j):
        term = lax.dot_general(
            weight[:, pl.ds(j * 256, 256)], s_rows[pl.ds(0, 1024), :],
            (((0,), (0,)), ((), ())), preferred_element_type=jnp.float32,
        ).astype(jnp.bfloat16)
        part_b[core, j] = term.reshape(2, 128, 1024)
        part_b_copy(j).start()

    def piece_of(ref, piece):
        return ref.at[pl.ds(piece * 64, 64), :]

    def slot_ready(slot):
        if slot < 4:
            part_a_arrival(slot).wait_recv()
        if slot >= 3:
            @pl.when(core != (slot - 3) // 5)
            def _():
                part_b_arrival((slot - 3) % 5).wait_recv()

    def sum_copy(which, slot, piece, src):
        into = INTO[which][piece][slot]
        return remote(
            piece_of(src, piece), piece_of(stage.at[slot], piece),
            r_send.at[slot * 2 + piece], r_recv.at[slot * 2 + piece],
            device(step(PLACE[slot], PLACE[into]), core),
        )

    def slot_terms(which, slot, piece):
        terms = []
        if slot < 4:
            terms += [part_a.at[0, slot, core], part_a.at[1, slot, core]]
        if slot >= 3:
            terms.append(part_b.at[(slot - 3) // 5, (slot - 3) % 5, core])
        for child in range(SLOTS):
            if INTO[which][piece][child] == slot:
                sum_copy(which, child, piece, stage.at[child]).wait_recv()
                terms.append(stage.at[child])
        return terms

    def added(terms, piece):
        return functools.reduce(
            lambda p, q: p + q, [piece_of(term, piece)[...].astype(jnp.float32) for term in terms]
        )

    def send_sum(slot, *pieces):
        def send(which):
            for piece in pieces:
                terms = slot_terms(which, slot, piece)
                if len(terms) == 1:
                    sum_copy(which, slot, piece, terms[0]).start()
                else:
                    piece_of(joined.at[slot], piece)[...] = added(terms, piece).astype(jnp.bfloat16)
                    sum_copy(which, slot, piece, joined.at[slot]).start()

        routes = [
            [(INTO[which][piece][slot], [c for c in range(SLOTS) if INTO[which][piece][c] == slot]) for piece in pieces]
            for which in (0, 1)
        ]
        if routes[0] == routes[1]:
            send(0)
        else:
            pl.when(core == 0)(lambda: send(0))
            pl.when(core == 1)(lambda: send(1))

    ready = set()
    for name in ORDER:
        if name[0] == "W":
            weights(int(name[1:]))
        elif name[0] == "A":
            rows_term(int(name[1:]))
            part_a_copy(int(name[1:])).start()
        elif name[0] == "B":
            columns_term(int(name[1:]))
        else:
            slot, piece = (int(n) for n in name.split("."))
            if slot not in ready:
                ready.add(slot)
                slot_ready(slot)
            send_sum(slot, piece)
    slot_ready(OWN)

    grad = logit_scale * jnp.concatenate(
        [added(slot_terms(0, OWN, piece), piece) for piece in (0, 1)], axis=0
    )
    student = unit[...]
    along = jnp.sum(student * grad, axis=1, keepdims=True)
    d_student = ((grad - student * along) / norm[:, 0:1]).astype(jnp.bfloat16)
    out[...] = lax.dot_general(d_student, proj[...], pair_dims, preferred_element_type=jnp.float32)

    for kind in range(4):
        for slot in range(SLOTS):
            if slot != OWN:
                row_copy(kind, OWN, slot).wait_send()
            if slot < 4:
                side_copy(kind, slot, half).wait_send()
            else:
                @pl.when(core == (1 if slot < OWN else 0))
                def _(kind=kind, slot=slot):
                    side_copy(kind, slot, half).wait_send()
    for index in range(9):
        for to_half in (0, 1):
            unless_own(index, to_half, lambda: stat_copy(index, to_half).wait_send())
        for of_core in (0, 1):
            if index == 4 and of_core == 1:
                pl.when(core == 0)(lambda: lse_copy(1, 4).wait_send())
            else:
                lse_copy(of_core, index).wait_send()
    for a in range(4):
        part_a_copy(a).wait_send()
    for j in range(COLS):
        part_b_copy(j).wait_send()
    for slot in range(SLOTS):
        if slot != OWN:
            for piece in (0, 1):
                sum_copy(0, slot, piece, joined.at[slot]).wait_send()


def per_device(features, teacher, proj):
    bf16, f32 = jnp.bfloat16, jnp.float32
    vmem = pl.BlockSpec(memory_space=pltpu.VMEM)
    dma = pltpu.SemaphoreType.DMA
    return pl.pallas_call(
        kernel,
        out_shape=jax.ShapeDtypeStruct((128, 1024), f32),
        in_specs=[pl.BlockSpec(memory_space=pl.ANY)] * 3,
        out_specs=vmem,
        scratch_shapes=[
            pltpu.VMEM((128, 1024), bf16),
            pltpu.VMEM((128, 1024), bf16),
            pltpu.VMEM((1024, 1024), bf16),
            pltpu.VMEM((SLOTS * 256, 1024), bf16),
            pltpu.VMEM((SLOTS * 256, 1024), bf16),
            pltpu.VMEM((1024, COLS * 256), f32),
            pltpu.VMEM((1024, COLS * 256), f32),
            pltpu.VMEM((1024, COLS * 256), bf16),
            pltpu.VMEM((2, 1024, 128), f32),
            pltpu.VMEM((2, 1024, 128), f32),
            pltpu.VMEM((2, 8, COLS * 256), f32),
            pltpu.VMEM((2, 8, COLS * 256), f32),
            pltpu.VMEM((9, 2, 8, 128), f32),
            pltpu.VMEM((18, 8, 128), f32),
            pltpu.VMEM((8, 128), f32),
            pltpu.VMEM((9, 2, 8, 128), f32),
            pltpu.VMEM((2, 1024, 128), f32),
            pltpu.VMEM((2, 4, 2, 128, 1024), bf16),
            pltpu.VMEM((2, COLS, 2, 128, 1024), bf16),
            pltpu.VMEM((SLOTS, 128, 1024), bf16),
            pltpu.VMEM((SLOTS, 128, 1024), bf16),
            pltpu.VMEM((128, 1024), f32),
            pltpu.VMEM((128, 128), f32),
            dma((4, SLOTS)), dma((4, SLOTS)), dma((4, SLOTS)), dma((4, SLOTS)),
            dma((18,)), dma((18,)), dma((18,)), dma((18,)),
            dma((4,)), dma((4,)), dma((COLS,)), dma((COLS,)), dma((2 * SLOTS,)), dma((2 * SLOTS,)), dma((3,)),
        ],
        compiler_params=pltpu.CompilerParams(
            collective_id=0, has_side_effects=True, vmem_limit_bytes=60 * 2**20
        ),
        cost_estimate=pl.CostEstimate(flops=9_000_000_000, bytes_accessed=4_000_000, transcendentals=9_000_000),
    )(features, teacher, proj)


def solution(mesh):
    in_specs = (P(("sub", "dp", "mp"), None), P(("sub", "dp", "mp"), None), P())
    out_specs = P(("sub", "dp", "mp"), None)
    return jax.shard_map(
        per_device, mesh=mesh, in_specs=in_specs, out_specs=out_specs, check_vma=False
    )
```

```python
import functools
import itertools

import jax
import jax.numpy as jnp
from jax import lax
from jax.experimental import pallas as pl
from jax.experimental.pallas import tpu as pltpu
from jax.sharding import PartitionSpec as P

MESH = pl.DeviceIdType.MESH
logit_scale = 100.0
epsilon = 1e-06
log2e = 1.4426950408889634
NEG = -1e30

PLACE = (
    (2, 3, 0), (1, 3, 0), (3, 3, 0), (0, 3, 0), (0, 0, 3), (0, 3, 1), (0, 1, 3), (0, 3, 2),
    (0, 0, 0), (0, 0, 1), (0, 1, 0), (0, 0, 2), (0, 1, 2),
)
SLOTS = 13
OWN = 8
COLS = 5
SHARE = ((0.5, 1.0, 1.0, 1.0, 0.5), (1.0, 1.0, 0.5, 1.0, 0.5))
FROM = (
    ((2, 3, 3, 8, 8, 9, 4, 5, -1, 8, 8, 9, 6), (1, 3, 3, 8, 8, 9, 4, 11, -1, 8, 8, 9, 6)),
    ((1, 3, 3, 8, 8, 3, 4, 11, -1, 8, 8, 4, 6), (2, 3, 3, 8, 8, 9, 4, 11, -1, 8, 8, 4, 11)),
    ((2, 3, 3, 8, 8, 9, 4, 5, -1, 8, 8, 4, 6), (2, 3, 3, 8, 8, 9, 4, 11, -1, 8, 8, 4, 11)),
    ((1, 3, 3, 8, 8, 3, 10, 5, -1, 8, 8, 9, 6), (1, 3, 3, 8, 8, 9, 4, 11, -1, 8, 8, 9, 11)),
)
FIRST = (
    "S3", "U10", "V9", "V10", "T9", "S9", "T10", "V3", "U4", "S4", "S10", "U9", "U3", "T4", "V4", "T3",
)
STEPS = (
    "S3", "U10", "U4", "V3", "T9", "V10", "U3", "V9", "T3", "T4", "S4", "S9", "V2", "S10", "S2", "V1", "S1", "U2",
    "T5", "V5", "U1", "U9", "V4", "s0", "U11", "U6", "s1", "T2", "V11", "T1", "S5", "V6", "T10", "T6", "T11", "s2",
    "t1", "t0", "S11", "S0", "V0", "S6", "U5", "t3", "U0", "U7", "T0", "s7", "t2", "s3", "t5", "s6", "s4", "t7",
    "t6", "V7", "U12", "S7", "V12", "S12", "T7", "T12", "s5", "t8", "s8", "t4",
)
INTO = (
    ((2, 3, 3, 8, 8, 9, 4, 5, -1, 8, 8, 9, 10), (2, 3, 3, 8, 8, 9, 4, 11, -1, 8, 8, 4, 11)),
    ((1, 3, 3, 8, 8, 9, 4, 5, -1, 8, 8, 9, 10), (1, 3, 3, 8, 8, 9, 4, 11, -1, 8, 8, 4, 6)),
)
ORDER = (
    "W0", "A0", "W1", "W2", "W3", "B4", "0.0", "A1", "7.0", "7.1", "0.1", "12.1", "A2", "B2", "12.0", "B3",
    "5.1", "6.0", "1.0", "2.0", "B1", "A3", "5.0", "1.1", "11.0", "11.1", "6.1", "B0", "2.1", "10.1", "4.0", "9.1", "3.0", "10.0", "9.0", "3.1", "4.1",
)
T, S = 0, 1


def step(a, b):
    return tuple((p - q) % 4 for p, q in zip(a, b))


NEIGHBOURS = ((1, 0, 0), (3, 0, 0), (0, 1, 0), (0, 3, 0), (0, 0, 1), (0, 0, 3))


def rows_of(slot, count=1):
    return pl.ds(slot * 256, count * 256)


def kernel(
    features_in, teacher_in, proj_in, out,
    features, teacher, proj,
    s_rows, t_rows, s_score, t_score, weight, top_parts, sum_parts, col_top, col_sum,
    stat_out, stat_in, lse_out, lse_in, lse_rows, part_a, part_b, stage, joined,
    unit, norm,
    g_send, g_recv, c_send, st_send, st_recv, l_send, l_recv,
    pa_send, pa_recv, pb_send, pb_recv, r_send, r_recv, in_sem,
):
    loads = [
        pltpu.make_async_copy(src, dst, in_sem.at[i])
        for i, (src, dst) in enumerate(((teacher_in, teacher), (features_in, features), (proj_in, proj)))
    ]
    for load in loads:
        load.start()

    sub, dp, mp = lax.axis_index("sub"), lax.axis_index("dp"), lax.axis_index("mp")
    x, y, z, core = sub * 2 + mp // 2, dp % 4, dp // 4, mp % 2
    other = 1 - core
    half = core * 128
    sibling = (sub, dp, (mp // 2) * 2 + other)
    rows_buf = (t_rows, s_rows)
    score_buf = (t_score, s_score)

    def device(move, to_core):
        ax, ay, az = (x + move[0]) % 4, (y + move[1]) % 4, (z + move[2]) % 4
        return (ax // 2, az * 4 + ay, (ax % 2) * 2 + to_core)

    barrier = pltpu.get_barrier_semaphore()
    for move in NEIGHBOURS:
        for to_core in (0, 1):
            pl.semaphore_signal(barrier, inc=1, device_id=device(move, to_core), device_id_type=MESH)
    pl.semaphore_signal(barrier, inc=1, device_id=sibling, device_id_type=MESH)

    def remote(src, dst, send, recv, target):
        return pltpu.make_async_remote_copy(
            src_ref=src, dst_ref=dst, send_sem=send, recv_sem=recv, device_id=target, device_id_type=MESH
        )

    def piece_rows(q, slot, which):
        return rows_buf[q // 2].at[pl.ds(slot * 256 + which + (q % 2) * 64, 64)]

    def user(slot):
        return 0 if slot < OWN else 1

    def straight(q, slot):
        return slot >= 4 and slot != OWN and slot not in FROM[q][1 - user(slot)]

    def row_copy(q, src_slot, slot):
        move = step(PLACE[src_slot], PLACE[slot])
        to_core, crossed = core, 0
        if straight(q, slot):
            to_core = user(slot)
            crossed = jnp.where(core == to_core, 0, 1)
        return remote(
            piece_rows(q, src_slot, half), piece_rows(q, slot, half),
            g_send.at[q, slot], g_recv.at[crossed, q, slot], device(move, to_core),
        )

    def side_copy(q, slot, which):
        piece = piece_rows(q, slot, which)
        return remote(piece, piece, c_send.at[q, slot], g_recv.at[1, q, slot], sibling)

    def to_side(q, slot):
        if slot < 4:
            side_copy(q, slot, half).start()
        elif not straight(q, slot):
            @pl.when(core != user(slot))
            def _():
                side_copy(q, slot, half).start()

    def start_rows(q, slot, children):
        for child in children:
            row_copy(q, slot, child).start()

    def arrive(q, slot):
        children = [[d for d in range(SLOTS) if FROM[q][which][d] == slot] for which in (0, 1)]
        if straight(q, slot):
            @pl.when(core == user(slot))
            def _():
                row_copy(q, OWN, slot).wait_recv()
                start_rows(q, slot, children[user(slot)])
            return
        row_copy(q, OWN, slot).wait_recv()
        if children[0] == children[1]:
            start_rows(q, slot, children[0])
        else:
            for which in (0, 1):
                if children[which]:
                    pl.when(core == which)(lambda: start_rows(q, slot, children[which]))
        to_side(q, slot)

    def side_wait(kind, *slots):
        for slot in slots:
            for q in (2 * kind, 2 * kind + 1):
                if slot < 4:
                    side_copy(q, slot, 128 - half).wait_recv()
                else:
                    @pl.when(core == user(slot))
                    def _(slot=slot, q=q):
                        side_copy(q, slot, 128 - half).wait_recv()

    own_rows = pl.ds(OWN * 256 + half, 128)
    loads[0].wait()
    values = teacher[...].astype(jnp.float32)
    t_rows[own_rows, :] = (
        values / jnp.sqrt(jnp.sum(values * values, axis=1, keepdims=True) + epsilon)
    ).astype(jnp.bfloat16)
    loads[1].wait()
    loads[2].wait()
    student = jnp.dot(features[...], proj[...], preferred_element_type=jnp.float32)
    length = jnp.sqrt(jnp.sum(student * student, axis=1, keepdims=True) + epsilon)
    student = student / length
    unit[...] = student
    norm[...] = jnp.broadcast_to(length, norm.shape)
    s_rows[own_rows, :] = student.astype(jnp.bfloat16)

    pl.semaphore_wait(barrier, 2 * len(NEIGHBOURS) + 1)
    for name in FIRST:
        start_rows("TUSV".index(name[0]), OWN, (int(name[1:]),))
    for q in range(4):
        to_side(q, OWN)

    for kind in (T, S):
        top_parts[kind] = jnp.full(top_parts.shape[1:], NEG, jnp.float32)
        sum_parts[kind] = jnp.zeros(sum_parts.shape[1:], jnp.float32)
        col_top[kind] = jnp.full(col_top.shape[1:], NEG, jnp.float32)
        col_sum[kind] = jnp.zeros(col_sum.shape[1:], jnp.float32)

    col_base = 3 + COLS * core
    pair_dims = (((1,), (1,)), ((), ()))
    lanes = lax.broadcasted_iota(jnp.int32, (256, 128), 1)

    def share(j):
        return jnp.where(core == 0, SHARE[0][j], SHARE[1][j]).astype(jnp.float32)

    shares = [share(j) for j in range(COLS)]

    def scores(*pieces):
        def product(kind, a0, na, j):
            buf = rows_buf[kind]
            score_buf[kind][pl.ds(a0 * 256, na * 256), pl.ds(j * 256, 256)] = lax.dot_general(
                buf[pl.ds(a0 * 256, na * 256), :],
                buf[pl.ds(pl.multiple_of((col_base + j) * 256, 256), 256), :],
                pair_dims, preferred_element_type=jnp.float32,
            ) * (logit_scale * log2e)
            if a0 <= 3 < a0 + na and j == 0:
                @pl.when(core == 0)
                def _():
                    tile = score_buf[kind][pl.ds(768, 256), pl.ds(0, 256)]
                    row = lax.broadcasted_iota(jnp.int32, (256, 256), 0)
                    col = lax.broadcasted_iota(jnp.int32, (256, 256), 1)
                    score_buf[kind][pl.ds(768, 256), pl.ds(0, 256)] = jnp.where(row == col, NEG, tile)

        def totals(kind, a0, na, j):
            cols = pl.ds(j * 256, 256)
            for a in range(a0, a0 + na):
                for i in range(4):
                    rows = pl.ds(a * 256 + i * 64, 64)
                    first = score_buf[kind][rows, pl.ds(j * 256, 128)]
                    second = score_buf[kind][rows, pl.ds(j * 256 + 128, 128)]
                    before = top_parts[kind, rows, :]
                    top = jnp.maximum(before, jnp.maximum(first, second))
                    total = jnp.exp2(first - top) + jnp.exp2(second - top)
                    sum_parts[kind, rows, :] = sum_parts[kind, rows, :] * jnp.exp2(before - top) + total * shares[j]
                    top_parts[kind, rows, :] = top
                tile = score_buf[kind][pl.ds(a * 256, 256), cols]
                top = jnp.max(tile, axis=0, keepdims=True)
                total = jnp.sum(jnp.exp2(tile - top), axis=0, keepdims=True)
                col_top[kind, a:a + 1, cols] = top
                col_sum[kind, a:a + 1, cols] = total

        product(*pieces[0])
        for last, piece in zip(pieces, pieces[1:]):
            totals(*last)
            product(*piece)
        totals(*pieces[-1])

    waited = set()

    def tiles(names):
        pieces = []
        for name in names:
            kind, n = "ts".index(name[0]), int(name[1:])
            a0, na, j = (1, 3, n) if n < 4 else (0, 1, n - 4) if n < 8 else (0, 4, 4)
            for slot in (*range(a0, a0 + na), 3 + j, 8 + j):
                if (kind, slot) not in waited:
                    waited.add((kind, slot))
                    side_wait(kind, slot)
            pieces.append((kind, a0, na, j))
        scores(*pieces)

    for upper, names in itertools.groupby(STEPS, str.isupper):
        if upper:
            for name in names:
                arrive("TUSV".index(name[0]), int(name[1:]))
        else:
            tiles(list(names))

    def row_totals(a):
        rows = pl.ds(a * 256, 256)
        packed = jnp.zeros((256, 128), jnp.float32)
        for kind in (T, S):
            parts = top_parts[kind, rows, :]
            top = jnp.max(parts, axis=1, keepdims=True)
            total = jnp.sum(sum_parts[kind, rows, :] * jnp.exp2(parts - top), axis=1, keepdims=True)
            packed = jnp.where(lanes == 2 * kind, top, packed)
            packed = jnp.where(lanes == 2 * kind + 1, total, packed)
        turned = packed.T
        stat_out[a, 0] = turned[0:8, 0:128]
        stat_out[a, 1] = turned[0:8, 128:256]
    def column_totals(j):
        cols = pl.ds(j * 256, 256)
        lines = []
        for kind in (T, S):
            parts = col_top[kind, :, cols]
            top = jnp.max(parts, axis=0, keepdims=True)
            total = jnp.sum(col_sum[kind, :, cols] * jnp.exp2(parts - top), axis=0, keepdims=True)
            lines += [top, total * shares[j]]
        lines.append(jnp.zeros((4, 256), jnp.float32))
        lines = jnp.concatenate(lines, axis=0)
        stat_out[4 + j, 0] = lines[:, 0:128]
        stat_out[4 + j, 1] = lines[:, 128:256]

    def place_at(index, of_core):
        if index < 4:
            return PLACE[index]
        first, second = PLACE[index - 1], PLACE[index + 4]
        return tuple(jnp.where(of_core == 0, p, q) for p, q in zip(first, second))

    def back(move):
        return tuple(4 - m for m in move)

    def stat_copy(index, to_half):
        return remote(
            stat_out.at[index, to_half], stat_in.at[core * 9 + index],
            st_send.at[index * 2 + to_half], st_recv.at[core * 9 + index],
            device(place_at(index, core), to_half),
        )

    def unless_own(index, to_half, action, instead=None):
        if index == 4 and to_half == 1:
            pl.when(core == 0)(action)
            if instead is not None:
                pl.when(core == 1)(instead)
        else:
            action()

    def keep_stat():
        stat_in[9 + 4] = stat_out[4, 1]

    for index in (8, 7, 0, 1, 2, 6, 5, 3, 4):
        if index < 4:
            row_totals(index)
        else:
            column_totals(index - 4)
        for to_half in (0, 1):
            unless_own(index, to_half, lambda: stat_copy(index, to_half).start(), keep_stat)

    def stat_arrival(source):
        return remote(
            stat_out.at[0, 0], stat_in.at[source], st_send.at[0], st_recv.at[source], sibling
        )

    for source in range(18):
        if source == 9 + 4:
            pl.when(core == 0)(lambda: stat_arrival(13).wait_recv())
        else:
            stat_arrival(source).wait_recv()

    lines = []
    for kind in (T, S):
        tops = stat_in[:, 2 * kind, :]
        top = jnp.max(tops, axis=0, keepdims=True)
        total = jnp.sum(stat_in[:, 2 * kind + 1, :] * jnp.exp2(tops - top), axis=0, keepdims=True)
        lines.append(top + jnp.log(total) * log2e)
    lines.append(jnp.zeros((6, 128), jnp.float32))
    lse_out[...] = jnp.concatenate(lines, axis=0)

    def lse_copy(of_core, index):
        return remote(
            lse_out, lse_in.at[index, core],
            l_send.at[of_core * 9 + index], l_recv.at[index * 2 + core],
            device(back(place_at(index, jnp.int32(of_core)) if index < 4 else PLACE[index - 1 + 5 * of_core]), of_core),
        )

    def lse_arrival(index, from_half):
        return remote(
            lse_out, lse_in.at[index, from_half], l_send.at[0], l_recv.at[index * 2 + from_half], sibling
        )

    def keep_lse():
        lse_in[4, 1] = lse_out[...]

    for index in (8, 0, 7, 1, 2, 6, 5, 3, 4):
        for of_core in (0, 1):
            if index == 4 and of_core == 1:
                pl.when(core == 0)(lambda: lse_copy(1, 4).start())
                pl.when(core == 1)(keep_lse)
            else:
                lse_copy(of_core, index).start()
    for index in range(9):
        for from_half in (0, 1):
            unless_own(index, from_half, lambda: lse_arrival(index, from_half).wait_recv())

    for a in range(4):
        lines = jnp.concatenate(
            [
                jnp.concatenate([lse_in[a, 0], lse_in[a, 1]], axis=1),
                jnp.zeros((120, 256), jnp.float32),
            ],
            axis=0,
        ).T
        for kind in (T, S):
            lse_rows[kind, pl.ds(a * 256, 256), :] = jnp.broadcast_to(lines[:, kind:kind + 1], (256, 128))

    def weights(a):
        for j in range(COLS):
            for side in (0, 1):
                for i in range(4):
                    rows = pl.ds(a * 256 + i * 64, 64)
                    cols = pl.ds(j * 256 + side * 128, 128)
                    s_tile, t_tile = s_score[rows, cols], t_score[rows, cols]
                    value = (
                        jnp.exp2(s_tile - lse_rows[S, rows, :])
                        + jnp.exp2(s_tile - lse_in[4 + j, side, S:S + 1, :])
                        - jnp.exp2(t_tile - lse_rows[T, rows, :])
                        - jnp.exp2(t_tile - lse_in[4 + j, side, T:T + 1, :])
                    )
                    weight[rows, cols] = (value * shares[j]).astype(jnp.bfloat16)

    def part_a_copy(a):
        piece = part_a.at[core, a, other]
        return remote(piece, piece, pa_send.at[a], pa_recv.at[a], sibling)

    def part_b_copy(j):
        piece = part_b.at[core, j, other]
        return remote(piece, piece, pb_send.at[j], pb_recv.at[j], sibling)

    def part_a_arrival(a):
        piece = part_a.at[other, a, core]
        return remote(piece, piece, pa_send.at[a], pa_recv.at[a], sibling)

    def part_b_arrival(j):
        piece = part_b.at[other, j, core]
        return remote(piece, piece, pb_send.at[j], pb_recv.at[j], sibling)

    def rows_term(a):
        term = jnp.dot(
            weight[pl.ds(a * 256, 256), :],
            s_rows[pl.ds(pl.multiple_of(col_base * 256, 256), COLS * 256), :],
            preferred_element_type=jnp.float32,
        ).astype(jnp.bfloat16)
        part_a[core, a] = term.reshape(2, 128, 1024)

    def columns_term(j):
        term = lax.dot_general(
            weight[:, pl.ds(j * 256, 256)], s_rows[pl.ds(0, 1024), :],
            (((0,), (0,)), ((), ())), preferred_element_type=jnp.float32,
        ).astype(jnp.bfloat16)
        part_b[core, j] = term.reshape(2, 128, 1024)
        part_b_copy(j).start()

    def piece_of(ref, piece):
        return ref.at[pl.ds(piece * 64, 64), :]

    def slot_ready(slot):
        if slot < 4:
            part_a_arrival(slot).wait_recv()
        if slot >= 3:
            @pl.when(core != (slot - 3) // 5)
            def _():
                part_b_arrival((slot - 3) % 5).wait_recv()

    def sum_copy(which, slot, piece, src):
        into = INTO[which][piece][slot]
        return remote(
            piece_of(src, piece), piece_of(stage.at[slot], piece),
            r_send.at[slot * 2 + piece], r_recv.at[slot * 2 + piece],
            device(step(PLACE[slot], PLACE[into]), core),
        )

    def slot_terms(which, slot, piece):
        terms = []
        if slot < 4:
            terms += [part_a.at[0, slot, core], part_a.at[1, slot, core]]
        if slot >= 3:
            terms.append(part_b.at[(slot - 3) // 5, (slot - 3) % 5, core])
        for child in range(SLOTS):
            if INTO[which][piece][child] == slot:
                sum_copy(which, child, piece, stage.at[child]).wait_recv()
                terms.append(stage.at[child])
        return terms

    def added(terms, piece):
        return functools.reduce(
            lambda p, q: p + q, [piece_of(term, piece)[...].astype(jnp.float32) for term in terms]
        )

    def send_sum(slot, *pieces):
        def send(which):
            for piece in pieces:
                terms = slot_terms(which, slot, piece)
                if len(terms) == 1:
                    sum_copy(which, slot, piece, terms[0]).start()
                else:
                    piece_of(joined.at[slot], piece)[...] = added(terms, piece).astype(jnp.bfloat16)
                    sum_copy(which, slot, piece, joined.at[slot]).start()

        routes = [
            [(INTO[which][piece][slot], [c for c in range(SLOTS) if INTO[which][piece][c] == slot]) for piece in pieces]
            for which in (0, 1)
        ]
        if routes[0] == routes[1]:
            send(0)
        else:
            pl.when(core == 0)(lambda: send(0))
            pl.when(core == 1)(lambda: send(1))

    ready = set()
    for name in ORDER:
        if name[0] == "W":
            weights(int(name[1:]))
        elif name[0] == "A":
            rows_term(int(name[1:]))
            part_a_copy(int(name[1:])).start()
        elif name[0] == "B":
            columns_term(int(name[1:]))
        else:
            slot, piece = (int(n) for n in name.split("."))
            if slot not in ready:
                ready.add(slot)
                slot_ready(slot)
            send_sum(slot, piece)
    slot_ready(OWN)

    grad = logit_scale * jnp.concatenate(
        [added(slot_terms(0, OWN, piece), piece) for piece in (0, 1)], axis=0
    )
    student = unit[...]
    along = jnp.sum(student * grad, axis=1, keepdims=True)
    d_student = ((grad - student * along) / norm[:, 0:1]).astype(jnp.bfloat16)
    out[...] = lax.dot_general(d_student, proj[...], pair_dims, preferred_element_type=jnp.float32)

    for kind in range(4):
        for slot in range(SLOTS):
            if slot != OWN:
                row_copy(kind, OWN, slot).wait_send()
            if slot < 4:
                side_copy(kind, slot, half).wait_send()
            elif not straight(kind, slot):
                @pl.when(core != user(slot))
                def _(kind=kind, slot=slot):
                    side_copy(kind, slot, half).wait_send()
    for index in range(9):
        for to_half in (0, 1):
            unless_own(index, to_half, lambda: stat_copy(index, to_half).wait_send())
        for of_core in (0, 1):
            if index == 4 and of_core == 1:
                pl.when(core == 0)(lambda: lse_copy(1, 4).wait_send())
            else:
                lse_copy(of_core, index).wait_send()
    for a in range(4):
        part_a_copy(a).wait_send()
    for j in range(COLS):
        part_b_copy(j).wait_send()
    for slot in range(SLOTS):
        if slot != OWN:
            for piece in (0, 1):
                sum_copy(0, slot, piece, joined.at[slot]).wait_send()


def per_device(features, teacher, proj):
    bf16, f32 = jnp.bfloat16, jnp.float32
    vmem = pl.BlockSpec(memory_space=pltpu.VMEM)
    dma = pltpu.SemaphoreType.DMA
    return pl.pallas_call(
        kernel,
        out_shape=jax.ShapeDtypeStruct((128, 1024), f32),
        in_specs=[pl.BlockSpec(memory_space=pl.ANY)] * 3,
        out_specs=vmem,
        scratch_shapes=[
            pltpu.VMEM((128, 1024), bf16),
            pltpu.VMEM((128, 1024), bf16),
            pltpu.VMEM((1024, 1024), bf16),
            pltpu.VMEM((SLOTS * 256, 1024), bf16),
            pltpu.VMEM((SLOTS * 256, 1024), bf16),
            pltpu.VMEM((1024, COLS * 256), f32),
            pltpu.VMEM((1024, COLS * 256), f32),
            pltpu.VMEM((1024, COLS * 256), bf16),
            pltpu.VMEM((2, 1024, 128), f32),
            pltpu.VMEM((2, 1024, 128), f32),
            pltpu.VMEM((2, 8, COLS * 256), f32),
            pltpu.VMEM((2, 8, COLS * 256), f32),
            pltpu.VMEM((9, 2, 8, 128), f32),
            pltpu.VMEM((18, 8, 128), f32),
            pltpu.VMEM((8, 128), f32),
            pltpu.VMEM((9, 2, 8, 128), f32),
            pltpu.VMEM((2, 1024, 128), f32),
            pltpu.VMEM((2, 4, 2, 128, 1024), bf16),
            pltpu.VMEM((2, COLS, 2, 128, 1024), bf16),
            pltpu.VMEM((SLOTS, 128, 1024), bf16),
            pltpu.VMEM((SLOTS, 128, 1024), bf16),
            pltpu.VMEM((128, 1024), f32),
            pltpu.VMEM((128, 128), f32),
            dma((4, SLOTS)), dma((2, 4, SLOTS)), dma((4, SLOTS)),
            dma((18,)), dma((18,)), dma((18,)), dma((18,)),
            dma((4,)), dma((4,)), dma((COLS,)), dma((COLS,)), dma((2 * SLOTS,)), dma((2 * SLOTS,)), dma((3,)),
        ],
        compiler_params=pltpu.CompilerParams(
            collective_id=0, has_side_effects=True, vmem_limit_bytes=60 * 2**20
        ),
        cost_estimate=pl.CostEstimate(flops=9_000_000_000, bytes_accessed=4_000_000, transcendentals=9_000_000),
    )(features, teacher, proj)


def solution(mesh):
    in_specs = (P(("sub", "dp", "mp"), None), P(("sub", "dp", "mp"), None), P())
    out_specs = P(("sub", "dp", "mp"), None)
    return jax.shard_map(
        per_device, mesh=mesh, in_specs=in_specs, out_specs=out_specs, check_vma=False
    )
```

```python
import functools
import itertools

import jax
import jax.numpy as jnp
from jax import lax
from jax.experimental import pallas as pl
from jax.experimental.pallas import tpu as pltpu
from jax.sharding import PartitionSpec as P

MESH = pl.DeviceIdType.MESH
logit_scale = 100.0
epsilon = 1e-06
log2e = 1.4426950408889634
NEG = -1e30

PLACE = (
    (2, 3, 0), (1, 3, 0), (3, 3, 0), (0, 3, 0), (0, 0, 3), (0, 3, 1), (0, 1, 3), (0, 3, 2),
    (0, 0, 0), (0, 0, 1), (0, 1, 0), (0, 0, 2), (0, 1, 2),
)
SLOTS = 13
OWN = 8
COLS = 5
SHARE = ((0.5, 1.0, 1.0, 1.0, 0.5), (1.0, 1.0, 0.5, 1.0, 0.5))
FROM = (
    ((2, 3, 3, 8, 8, 9, 4, 5, -1, 8, 8, 9, 6), (1, 3, 3, 8, 8, 9, 4, 11, -1, 8, 8, 9, 6)),
    ((1, 3, 3, 8, 8, 3, 4, 11, -1, 8, 8, 4, 6), (2, 3, 3, 8, 8, 9, 4, 11, -1, 8, 8, 4, 11)),
    ((2, 3, 3, 8, 8, 9, 4, 5, -1, 8, 8, 4, 6), (2, 3, 3, 8, 8, 9, 4, 11, -1, 8, 8, 4, 11)),
    ((1, 3, 3, 8, 8, 3, 10, 5, -1, 8, 8, 9, 6), (1, 3, 3, 8, 8, 9, 4, 11, -1, 8, 8, 9, 11)),
)
FIRST = (
    "S3", "U10", "V9", "V10", "T9", "S9", "T10", "V3", "U4", "S4", "S10", "U9", "U3", "T4", "V4", "T3",
)
STEPS = (
    "S3", "U10", "U4", "V3", "T9", "V10", "U3", "V9", "T3", "T4", "S4", "S9", "V2", "S10", "S2", "V1", "S1", "U2",
    "T5", "V5", "U1", "U9", "V4", "s0", "U11", "U6", "s1", "T2", "V11", "T1", "S5", "V6", "T10", "T6", "T11", "s2",
    "t1", "t0", "S11", "S0", "V0", "S6", "U5", "t3", "U0", "U7", "T0", "s7", "t2", "s3", "t5", "s6", "s4", "t7",
    "t6", "V7", "U12", "S7", "V12", "S12", "T7", "T12", "s5", "t8", "s8", "t4",
)
INTO = (
    ((1, 3, 3, 8, 8, 9, 4, 5, -1, 8, 8, 9, 11), (1, 3, 3, 8, 8, 9, 4, 11, -1, 8, 8, 4, 10)),
    ((3, 3, 3, 8, 8, 9, 10, 5, -1, 8, 8, 9, 10), (1, 3, 3, 8, 8, 9, 4, 11, -1, 8, 8, 4, 11)),
)
ORDER = (
    "W0", "A0", "W1", "W2", "W3", "B4", "0.0", "A2", "7.1", "7.0", "0.1", "12.0", "12.1", "A1", "B2", "B3", "2.0", "5.1",
    "6.0", "2.1", "1.0", "B1", "6.1", "A3", "5.0", "11.1", "11.0", "B0", "1.1", "10.0", "9.1", "3.0", "4.0", "4.1", "10.1", "9.0",
    "3.1",
)
T, S = 0, 1


def step(a, b):
    return tuple((p - q) % 4 for p, q in zip(a, b))


NEIGHBOURS = ((1, 0, 0), (3, 0, 0), (0, 1, 0), (0, 3, 0), (0, 0, 1), (0, 0, 3))


def rows_of(slot, count=1):
    return pl.ds(slot * 256, count * 256)


def kernel(
    features_in, teacher_in, proj_in, out,
    features, teacher, proj,
    s_rows, t_rows, s_score, t_score, weight, top_parts, sum_parts, col_top, col_sum,
    stat_out, stat_in, lse_out, lse_in, lse_rows, part_a, part_b, stage, joined,
    unit, norm,
    g_send, g_recv, c_send, st_send, st_recv, l_send, l_recv,
    pa_send, pa_recv, pb_send, pb_recv, r_send, r_recv, in_sem,
):
    loads = [
        pltpu.make_async_copy(src, dst, in_sem.at[i])
        for i, (src, dst) in enumerate(((teacher_in, teacher), (features_in, features), (proj_in, proj)))
    ]
    for load in loads:
        load.start()

    sub, dp, mp = lax.axis_index("sub"), lax.axis_index("dp"), lax.axis_index("mp")
    x, y, z, core = sub * 2 + mp // 2, dp % 4, dp // 4, mp % 2
    other = 1 - core
    half = core * 128
    sibling = (sub, dp, (mp // 2) * 2 + other)
    rows_buf = (t_rows, s_rows)
    score_buf = (t_score, s_score)

    def device(move, to_core):
        ax, ay, az = (x + move[0]) % 4, (y + move[1]) % 4, (z + move[2]) % 4
        return (ax // 2, az * 4 + ay, (ax % 2) * 2 + to_core)

    barrier = pltpu.get_barrier_semaphore()
    for move in NEIGHBOURS:
        pl.semaphore_signal(barrier, inc=1, device_id=device(move, core), device_id_type=MESH)
    pl.semaphore_signal(barrier, inc=1, device_id=sibling, device_id_type=MESH)

    def remote(src, dst, send, recv, target):
        return pltpu.make_async_remote_copy(
            src_ref=src, dst_ref=dst, send_sem=send, recv_sem=recv, device_id=target, device_id_type=MESH
        )

    def piece_rows(q, slot, which):
        return rows_buf[q // 2].at[pl.ds(slot * 256 + which + (q % 2) * 64, 64)]

    def user(slot):
        return 0 if slot < OWN else 1

    def straight(q, slot):
        source = FROM[q][1 - user(slot)]
        return slot >= 4 and slot != OWN and source[slot] != OWN and slot not in source

    def row_copy(q, src_slot, slot):
        move = step(PLACE[src_slot], PLACE[slot])
        to_core, crossed = core, 0
        if straight(q, slot):
            to_core = user(slot)
            crossed = jnp.where(core == to_core, 0, 1)
        return remote(
            piece_rows(q, src_slot, half), piece_rows(q, slot, half),
            g_send.at[q, slot], g_recv.at[crossed, q, slot], device(move, to_core),
        )

    def side_copy(q, slot, which):
        piece = piece_rows(q, slot, which)
        return remote(piece, piece, c_send.at[q, slot], g_recv.at[1, q, slot], sibling)

    def to_side(q, slot):
        if slot < 4:
            side_copy(q, slot, half).start()
        elif not straight(q, slot):
            @pl.when(core != user(slot))
            def _():
                side_copy(q, slot, half).start()

    def start_rows(q, slot, children):
        for child in children:
            row_copy(q, slot, child).start()

    def arrive(q, slot):
        children = [[d for d in range(SLOTS) if FROM[q][which][d] == slot] for which in (0, 1)]
        if straight(q, slot):
            @pl.when(core == user(slot))
            def _():
                row_copy(q, OWN, slot).wait_recv()
                start_rows(q, slot, children[user(slot)])
            return
        row_copy(q, OWN, slot).wait_recv()
        if children[0] == children[1]:
            start_rows(q, slot, children[0])
        else:
            for which in (0, 1):
                if children[which]:
                    pl.when(core == which)(lambda: start_rows(q, slot, children[which]))
        to_side(q, slot)

    def side_wait(kind, *slots):
        for slot in slots:
            for q in (2 * kind, 2 * kind + 1):
                if slot < 4:
                    side_copy(q, slot, 128 - half).wait_recv()
                else:
                    @pl.when(core == user(slot))
                    def _(slot=slot, q=q):
                        side_copy(q, slot, 128 - half).wait_recv()

    own_rows = pl.ds(OWN * 256 + half, 128)
    loads[0].wait()
    values = teacher[...].astype(jnp.float32)
    t_rows[own_rows, :] = (
        values / jnp.sqrt(jnp.sum(values * values, axis=1, keepdims=True) + epsilon)
    ).astype(jnp.bfloat16)
    loads[1].wait()
    loads[2].wait()
    student = jnp.dot(features[...], proj[...], preferred_element_type=jnp.float32)
    length = jnp.sqrt(jnp.sum(student * student, axis=1, keepdims=True) + epsilon)
    student = student / length
    unit[...] = student
    norm[...] = jnp.broadcast_to(length, norm.shape)
    s_rows[own_rows, :] = student.astype(jnp.bfloat16)

    pl.semaphore_wait(barrier, len(NEIGHBOURS) + 1)
    for name in FIRST:
        start_rows("TUSV".index(name[0]), OWN, (int(name[1:]),))
    for q in range(4):
        to_side(q, OWN)

    for kind in (T, S):
        top_parts[kind] = jnp.full(top_parts.shape[1:], NEG, jnp.float32)
        sum_parts[kind] = jnp.zeros(sum_parts.shape[1:], jnp.float32)
        col_top[kind] = jnp.full(col_top.shape[1:], NEG, jnp.float32)
        col_sum[kind] = jnp.zeros(col_sum.shape[1:], jnp.float32)

    col_base = 3 + COLS * core
    pair_dims = (((1,), (1,)), ((), ()))
    lanes = lax.broadcasted_iota(jnp.int32, (256, 128), 1)

    def share(j):
        return jnp.where(core == 0, SHARE[0][j], SHARE[1][j]).astype(jnp.float32)

    shares = [share(j) for j in range(COLS)]

    def scores(*pieces):
        def product(kind, a0, na, j):
            buf = rows_buf[kind]
            score_buf[kind][pl.ds(a0 * 256, na * 256), pl.ds(j * 256, 256)] = lax.dot_general(
                buf[pl.ds(a0 * 256, na * 256), :],
                buf[pl.ds(pl.multiple_of((col_base + j) * 256, 256), 256), :],
                pair_dims, preferred_element_type=jnp.float32,
            ) * (logit_scale * log2e)
            if a0 <= 3 < a0 + na and j == 0:
                @pl.when(core == 0)
                def _():
                    tile = score_buf[kind][pl.ds(768, 256), pl.ds(0, 256)]
                    row = lax.broadcasted_iota(jnp.int32, (256, 256), 0)
                    col = lax.broadcasted_iota(jnp.int32, (256, 256), 1)
                    score_buf[kind][pl.ds(768, 256), pl.ds(0, 256)] = jnp.where(row == col, NEG, tile)

        def totals(kind, a0, na, j):
            cols = pl.ds(j * 256, 256)
            for a in range(a0, a0 + na):
                for i in range(4):
                    rows = pl.ds(a * 256 + i * 64, 64)
                    first = score_buf[kind][rows, pl.ds(j * 256, 128)]
                    second = score_buf[kind][rows, pl.ds(j * 256 + 128, 128)]
                    before = top_parts[kind, rows, :]
                    top = jnp.maximum(before, jnp.maximum(first, second))
                    total = jnp.exp2(first - top) + jnp.exp2(second - top)
                    sum_parts[kind, rows, :] = sum_parts[kind, rows, :] * jnp.exp2(before - top) + total * shares[j]
                    top_parts[kind, rows, :] = top
                tile = score_buf[kind][pl.ds(a * 256, 256), cols]
                top = jnp.max(tile, axis=0, keepdims=True)
                total = jnp.sum(jnp.exp2(tile - top), axis=0, keepdims=True)
                col_top[kind, a:a + 1, cols] = top
                col_sum[kind, a:a + 1, cols] = total

        product(*pieces[0])
        for last, piece in zip(pieces, pieces[1:]):
            totals(*last)
            product(*piece)
        totals(*pieces[-1])

    waited = set()

    def tiles(names):
        pieces = []
        for name in names:
            kind, n = "ts".index(name[0]), int(name[1:])
            a0, na, j = (1, 3, n) if n < 4 else (0, 1, n - 4) if n < 8 else (0, 4, 4)
            for slot in (*range(a0, a0 + na), 3 + j, 8 + j):
                if (kind, slot) not in waited:
                    waited.add((kind, slot))
                    side_wait(kind, slot)
            pieces.append((kind, a0, na, j))
        scores(*pieces)

    for upper, names in itertools.groupby(STEPS, str.isupper):
        if upper:
            for name in names:
                arrive("TUSV".index(name[0]), int(name[1:]))
        else:
            tiles(list(names))

    def row_totals(a):
        rows = pl.ds(a * 256, 256)
        packed = jnp.zeros((256, 128), jnp.float32)
        for kind in (T, S):
            parts = top_parts[kind, rows, :]
            top = jnp.max(parts, axis=1, keepdims=True)
            total = jnp.sum(sum_parts[kind, rows, :] * jnp.exp2(parts - top), axis=1, keepdims=True)
            packed = jnp.where(lanes == 2 * kind, top, packed)
            packed = jnp.where(lanes == 2 * kind + 1, total, packed)
        turned = packed.T
        stat_out[a, 0] = turned[0:8, 0:128]
        stat_out[a, 1] = turned[0:8, 128:256]
    def column_totals(j):
        cols = pl.ds(j * 256, 256)
        lines = []
        for kind in (T, S):
            parts = col_top[kind, :, cols]
            top = jnp.max(parts, axis=0, keepdims=True)
            total = jnp.sum(col_sum[kind, :, cols] * jnp.exp2(parts - top), axis=0, keepdims=True)
            lines += [top, total * shares[j]]
        lines.append(jnp.zeros((4, 256), jnp.float32))
        lines = jnp.concatenate(lines, axis=0)
        stat_out[4 + j, 0] = lines[:, 0:128]
        stat_out[4 + j, 1] = lines[:, 128:256]

    def place_at(index, of_core):
        if index < 4:
            return PLACE[index]
        first, second = PLACE[index - 1], PLACE[index + 4]
        return tuple(jnp.where(of_core == 0, p, q) for p, q in zip(first, second))

    def back(move):
        return tuple(4 - m for m in move)

    def stat_copy(index, to_half):
        return remote(
            stat_out.at[index, to_half], stat_in.at[core * 9 + index],
            st_send.at[index * 2 + to_half], st_recv.at[core * 9 + index],
            device(place_at(index, core), to_half),
        )

    def unless_own(index, to_half, action, instead=None):
        if index == 4 and to_half == 1:
            pl.when(core == 0)(action)
            if instead is not None:
                pl.when(core == 1)(instead)
        else:
            action()

    def keep_stat():
        stat_in[9 + 4] = stat_out[4, 1]

    for index in (8, 7, 0, 1, 2, 6, 5, 3, 4):
        if index < 4:
            row_totals(index)
        else:
            column_totals(index - 4)
        for to_half in (0, 1):
            unless_own(index, to_half, lambda: stat_copy(index, to_half).start(), keep_stat)

    def stat_arrival(source):
        return remote(
            stat_out.at[0, 0], stat_in.at[source], st_send.at[0], st_recv.at[source], sibling
        )

    for source in range(18):
        if source == 9 + 4:
            pl.when(core == 0)(lambda: stat_arrival(13).wait_recv())
        else:
            stat_arrival(source).wait_recv()

    lines = []
    for kind in (T, S):
        tops = stat_in[:, 2 * kind, :]
        top = jnp.max(tops, axis=0, keepdims=True)
        total = jnp.sum(stat_in[:, 2 * kind + 1, :] * jnp.exp2(tops - top), axis=0, keepdims=True)
        lines.append(top + jnp.log(total) * log2e)
    lines.append(jnp.zeros((6, 128), jnp.float32))
    lse_out[...] = jnp.concatenate(lines, axis=0)

    def lse_copy(of_core, index):
        return remote(
            lse_out, lse_in.at[index, core],
            l_send.at[of_core * 9 + index], l_recv.at[index * 2 + core],
            device(back(place_at(index, jnp.int32(of_core)) if index < 4 else PLACE[index - 1 + 5 * of_core]), of_core),
        )

    def lse_arrival(index, from_half):
        return remote(
            lse_out, lse_in.at[index, from_half], l_send.at[0], l_recv.at[index * 2 + from_half], sibling
        )

    def keep_lse():
        lse_in[4, 1] = lse_out[...]

    for index in (8, 0, 7, 1, 2, 6, 5, 3, 4):
        for of_core in (0, 1):
            if index == 4 and of_core == 1:
                pl.when(core == 0)(lambda: lse_copy(1, 4).start())
                pl.when(core == 1)(keep_lse)
            else:
                lse_copy(of_core, index).start()
    for index in range(9):
        for from_half in (0, 1):
            unless_own(index, from_half, lambda: lse_arrival(index, from_half).wait_recv())

    for a in range(4):
        lines = jnp.concatenate(
            [
                jnp.concatenate([lse_in[a, 0], lse_in[a, 1]], axis=1),
                jnp.zeros((120, 256), jnp.float32),
            ],
            axis=0,
        ).T
        for kind in (T, S):
            lse_rows[kind, pl.ds(a * 256, 256), :] = jnp.broadcast_to(lines[:, kind:kind + 1], (256, 128))

    def weights(a):
        for j in range(COLS):
            for side in (0, 1):
                for i in range(4):
                    rows = pl.ds(a * 256 + i * 64, 64)
                    cols = pl.ds(j * 256 + side * 128, 128)
                    s_tile, t_tile = s_score[rows, cols], t_score[rows, cols]
                    value = (
                        jnp.exp2(s_tile - lse_rows[S, rows, :])
                        + jnp.exp2(s_tile - lse_in[4 + j, side, S:S + 1, :])
                        - jnp.exp2(t_tile - lse_rows[T, rows, :])
                        - jnp.exp2(t_tile - lse_in[4 + j, side, T:T + 1, :])
                    )
                    weight[rows, cols] = (value * shares[j]).astype(jnp.bfloat16)

    def part_a_copy(a):
        piece = part_a.at[core, a, other]
        return remote(piece, piece, pa_send.at[a], pa_recv.at[a], sibling)

    def part_b_copy(j):
        piece = part_b.at[core, j, other]
        return remote(piece, piece, pb_send.at[j], pb_recv.at[j], sibling)

    def part_a_arrival(a):
        piece = part_a.at[other, a, core]
        return remote(piece, piece, pa_send.at[a], pa_recv.at[a], sibling)

    def part_b_arrival(j):
        piece = part_b.at[other, j, core]
        return remote(piece, piece, pb_send.at[j], pb_recv.at[j], sibling)

    def rows_term(a):
        term = jnp.dot(
            weight[pl.ds(a * 256, 256), :],
            s_rows[pl.ds(pl.multiple_of(col_base * 256, 256), COLS * 256), :],
            preferred_element_type=jnp.float32,
        ).astype(jnp.bfloat16)
        part_a[core, a] = term.reshape(2, 128, 1024)

    def columns_term(j):
        term = lax.dot_general(
            weight[:, pl.ds(j * 256, 256)], s_rows[pl.ds(0, 1024), :],
            (((0,), (0,)), ((), ())), preferred_element_type=jnp.float32,
        ).astype(jnp.bfloat16)
        part_b[core, j] = term.reshape(2, 128, 1024)
        part_b_copy(j).start()

    def piece_of(ref, piece):
        return ref.at[pl.ds(piece * 64, 64), :]

    def slot_ready(slot):
        if slot < 4:
            part_a_arrival(slot).wait_recv()
        if slot >= 3:
            @pl.when(core != (slot - 3) // 5)
            def _():
                part_b_arrival((slot - 3) % 5).wait_recv()

    def sum_copy(which, slot, piece, src):
        into = INTO[which][piece][slot]
        return remote(
            piece_of(src, piece), piece_of(stage.at[slot], piece),
            r_send.at[slot * 2 + piece], r_recv.at[slot * 2 + piece],
            device(step(PLACE[slot], PLACE[into]), core),
        )

    def slot_terms(which, slot, piece):
        terms = []
        if slot < 4:
            terms += [part_a.at[0, slot, core], part_a.at[1, slot, core]]
        if slot >= 3:
            terms.append(part_b.at[(slot - 3) // 5, (slot - 3) % 5, core])
        for child in range(SLOTS):
            if INTO[which][piece][child] == slot:
                sum_copy(which, child, piece, stage.at[child]).wait_recv()
                terms.append(stage.at[child])
        return terms

    def added(terms, piece):
        return functools.reduce(
            lambda p, q: p + q, [piece_of(term, piece)[...].astype(jnp.float32) for term in terms]
        )

    def send_sum(slot, *pieces):
        def send(which):
            for piece in pieces:
                terms = slot_terms(which, slot, piece)
                if len(terms) == 1:
                    sum_copy(which, slot, piece, terms[0]).start()
                else:
                    piece_of(joined.at[slot], piece)[...] = added(terms, piece).astype(jnp.bfloat16)
                    sum_copy(which, slot, piece, joined.at[slot]).start()

        routes = [
            [(INTO[which][piece][slot], [c for c in range(SLOTS) if INTO[which][piece][c] == slot]) for piece in pieces]
            for which in (0, 1)
        ]
        if routes[0] == routes[1]:
            send(0)
        else:
            pl.when(core == 0)(lambda: send(0))
            pl.when(core == 1)(lambda: send(1))

    ready = set()
    for at, name in enumerate(ORDER):
        if name[0] == "W":
            weights(int(name[1:]))
            if ORDER[at - 1][0] == "A":
                part_a_copy(int(ORDER[at - 1][1:])).start()
        elif name[0] == "A":
            rows_term(int(name[1:]))
            if ORDER[at + 1][0] != "W":
                part_a_copy(int(name[1:])).start()
        elif name[0] == "B":
            columns_term(int(name[1:]))
        else:
            slot, piece = (int(n) for n in name.split("."))
            if slot not in ready:
                ready.add(slot)
                slot_ready(slot)
            send_sum(slot, piece)
    slot_ready(OWN)

    for piece in (0, 1):
        rows = pl.ds(piece * 64, 64)
        grad = logit_scale * added(slot_terms(0, OWN, piece), piece)
        student = unit[rows, :]
        along = jnp.sum(student * grad, axis=1, keepdims=True)
        out[rows, :] = ((grad - student * along) / norm[rows, 0:1]).astype(jnp.bfloat16)

    for kind in range(4):
        for slot in range(SLOTS):
            if slot != OWN:
                row_copy(kind, OWN, slot).wait_send()
            if slot < 4:
                side_copy(kind, slot, half).wait_send()
            elif not straight(kind, slot):
                @pl.when(core != user(slot))
                def _(kind=kind, slot=slot):
                    side_copy(kind, slot, half).wait_send()
    for index in range(9):
        for to_half in (0, 1):
            unless_own(index, to_half, lambda: stat_copy(index, to_half).wait_send())
        for of_core in (0, 1):
            if index == 4 and of_core == 1:
                pl.when(core == 0)(lambda: lse_copy(1, 4).wait_send())
            else:
                lse_copy(of_core, index).wait_send()
    for a in range(4):
        part_a_copy(a).wait_send()
    for j in range(COLS):
        part_b_copy(j).wait_send()
    for slot in range(SLOTS):
        if slot != OWN:
            for piece in (0, 1):
                sum_copy(0, slot, piece, joined.at[slot]).wait_send()


def per_device(features, teacher, proj):
    bf16, f32 = jnp.bfloat16, jnp.float32
    vmem = pl.BlockSpec(memory_space=pltpu.VMEM)
    dma = pltpu.SemaphoreType.DMA
    d_student = pl.pallas_call(
        kernel,
        out_shape=jax.ShapeDtypeStruct((128, 1024), bf16),
        in_specs=[pl.BlockSpec(memory_space=pl.ANY)] * 3,
        out_specs=vmem,
        scratch_shapes=[
            pltpu.VMEM((128, 1024), bf16),
            pltpu.VMEM((128, 1024), bf16),
            pltpu.VMEM((1024, 1024), bf16),
            pltpu.VMEM((SLOTS * 256, 1024), bf16),
            pltpu.VMEM((SLOTS * 256, 1024), bf16),
            pltpu.VMEM((1024, COLS * 256), f32),
            pltpu.VMEM((1024, COLS * 256), f32),
            pltpu.VMEM((1024, COLS * 256), bf16),
            pltpu.VMEM((2, 1024, 128), f32),
            pltpu.VMEM((2, 1024, 128), f32),
            pltpu.VMEM((2, 8, COLS * 256), f32),
            pltpu.VMEM((2, 8, COLS * 256), f32),
            pltpu.VMEM((9, 2, 8, 128), f32),
            pltpu.VMEM((18, 8, 128), f32),
            pltpu.VMEM((8, 128), f32),
            pltpu.VMEM((9, 2, 8, 128), f32),
            pltpu.VMEM((2, 1024, 128), f32),
            pltpu.VMEM((2, 4, 2, 128, 1024), bf16),
            pltpu.VMEM((2, COLS, 2, 128, 1024), bf16),
            pltpu.VMEM((SLOTS, 128, 1024), bf16),
            pltpu.VMEM((SLOTS, 128, 1024), bf16),
            pltpu.VMEM((128, 1024), f32),
            pltpu.VMEM((128, 128), f32),
            dma((4, SLOTS)), dma((2, 4, SLOTS)), dma((4, SLOTS)),
            dma((18,)), dma((18,)), dma((18,)), dma((18,)),
            dma((4,)), dma((4,)), dma((COLS,)), dma((COLS,)), dma((2 * SLOTS,)), dma((2 * SLOTS,)), dma((3,)),
        ],
        compiler_params=pltpu.CompilerParams(
            collective_id=0, has_side_effects=True, vmem_limit_bytes=60 * 2**20
        ),
        cost_estimate=pl.CostEstimate(flops=9_000_000_000, bytes_accessed=4_000_000, transcendentals=9_000_000),
    )(features, teacher, proj)
    return lax.dot_general(
        d_student, proj, (((1,), (1,)), ((), ())), preferred_element_type=f32
    )


def solution(mesh):
    in_specs = (P(("sub", "dp", "mp"), None), P(("sub", "dp", "mp"), None), P())
    out_specs = P(("sub", "dp", "mp"), None)
    return jax.shard_map(
        per_device, mesh=mesh, in_specs=in_specs, out_specs=out_specs, check_vma=False
    )
```

```python
import functools
import itertools

import jax
import jax.numpy as jnp
from jax import lax
from jax.experimental import pallas as pl
from jax.experimental.pallas import tpu as pltpu
from jax.sharding import PartitionSpec as P

MESH = pl.DeviceIdType.MESH
logit_scale = 100.0
epsilon = 1e-06
log2e = 1.4426950408889634
NEG = -1e30

PLACE = (
    (2, 3, 0), (1, 3, 0), (3, 3, 0), (0, 3, 0), (0, 0, 3), (0, 3, 1), (0, 1, 3), (0, 3, 2),
    (0, 0, 0), (0, 0, 1), (0, 1, 0), (0, 0, 2), (0, 1, 2),
)
SLOTS = 13
OWN = 8
COLS = 5
SHARE = ((0.5, 1.0, 1.0, 1.0, 0.5), (1.0, 1.0, 0.5, 1.0, 0.5))
FROM = (
    ((2, 3, 3, 8, 8, 9, 4, 5, -1, 8, 8, 9, 6), (1, 3, 3, 8, 8, 9, 4, 11, -1, 8, 8, 9, 6)),
    ((1, 3, 3, 8, 8, 3, 4, 11, -1, 8, 8, 4, 6), (2, 3, 3, 8, 8, 9, 4, 11, -1, 8, 8, 4, 11)),
    ((2, 3, 3, 8, 8, 9, 4, 5, -1, 8, 8, 4, 6), (2, 3, 3, 8, 8, 9, 4, 11, -1, 8, 8, 4, 11)),
    ((1, 3, 3, 8, 8, 3, 10, 5, -1, 8, 8, 9, 6), (1, 3, 3, 8, 8, 9, 4, 11, -1, 8, 8, 9, 11)),
)
FIRST = (
    "S3", "U10", "V9", "V10", "T9", "S9", "T10", "V3", "U4", "S4", "S10", "U9", "U3", "T4", "V4", "T3",
)
STEPS = (
    "S3", "U10", "U4", "V3", "T9", "V10", "U3", "V9", "T3", "T4", "S4", "S9", "V2", "S10", "S2", "V1", "S1", "U2",
    "T5", "V5", "U1", "U9", "V4", "s0", "U11", "U6", "s1", "T2", "V11", "T1", "S5", "V6", "T10", "T6", "T11", "s2",
    "t1", "t0", "S11", "S0", "V0", "S6", "U5", "t3", "U0", "U7", "T0", "s7", "t2", "s3", "t5", "s6", "s4", "t7",
    "t6", "V7", "U12", "S7", "V12", "S12", "T7", "T12", "s5", "t8", "s8", "t4",
)
INTO = (
    ((1, 3, 3, 8, 8, 9, 4, 5, -1, 8, 8, 9, 11), (1, 3, 3, 8, 8, 9, 4, 11, -1, 8, 8, 4, 10)),
    ((3, 3, 3, 8, 8, 9, 10, 5, -1, 8, 8, 9, 10), (1, 3, 3, 8, 8, 9, 4, 11, -1, 8, 8, 4, 11)),
)
ORDER = (
    "W0", "A0", "W1", "W2", "W3", "B4", "0.0", "A2", "7.1", "7.0", "0.1", "12.0", "12.1", "A1", "B2", "B3", "2.0", "5.1",
    "6.0", "2.1", "1.0", "B1", "6.1", "A3", "5.0", "11.1", "11.0", "B0", "1.1", "10.0", "9.1", "3.0", "4.0", "4.1", "10.1", "9.0",
    "3.1",
)
T, S = 0, 1


def step(a, b):
    return tuple((p - q) % 4 for p, q in zip(a, b))


NEIGHBOURS = ((1, 0, 0), (3, 0, 0), (0, 1, 0), (0, 3, 0), (0, 0, 1), (0, 0, 3))


def rows_of(slot, count=1):
    return pl.ds(slot * 256, count * 256)


def kernel(
    features_in, teacher_in, proj_in, out,
    features, teacher, proj,
    s_rows, t_rows, s_score, t_score, weight, top_parts, sum_parts, col_top, col_sum,
    stat_out, stat_in, lse_out, lse_in, lse_rows, part_a, part_b, stage, joined,
    unit, norm,
    g_send, g_recv, c_send, st_send, st_recv, l_send, l_recv,
    pa_send, pa_recv, pb_send, pb_recv, r_send, r_recv, in_sem,
):
    loads = [
        pltpu.make_async_copy(src, dst, in_sem.at[i])
        for i, (src, dst) in enumerate(((teacher_in, teacher), (features_in, features), (proj_in, proj)))
    ]
    for load in loads:
        load.start()

    sub, dp, mp = lax.axis_index("sub"), lax.axis_index("dp"), lax.axis_index("mp")
    x, y, z, core = sub * 2 + mp // 2, dp % 4, dp // 4, mp % 2
    other = 1 - core
    half = core * 128
    sibling = (sub, dp, (mp // 2) * 2 + other)
    rows_buf = (t_rows, s_rows)
    score_buf = (t_score, s_score)

    def device(move, to_core):
        ax, ay, az = (x + move[0]) % 4, (y + move[1]) % 4, (z + move[2]) % 4
        return (ax // 2, az * 4 + ay, (ax % 2) * 2 + to_core)

    barrier = pltpu.get_barrier_semaphore()
    for move in NEIGHBOURS:
        pl.semaphore_signal(barrier, inc=1, device_id=device(move, core), device_id_type=MESH)
    pl.semaphore_signal(barrier, inc=1, device_id=sibling, device_id_type=MESH)

    def remote(src, dst, send, recv, target):
        return pltpu.make_async_remote_copy(
            src_ref=src, dst_ref=dst, send_sem=send, recv_sem=recv, device_id=target, device_id_type=MESH
        )

    def piece_rows(q, slot, which):
        return rows_buf[q // 2].at[pl.ds(slot * 256 + which + (q % 2) * 64, 64)]

    def user(slot):
        return 0 if slot < OWN else 1

    def straight(q, slot):
        source = FROM[q][1 - user(slot)]
        return slot >= 4 and slot != OWN and source[slot] != OWN and slot not in source

    def row_copy(q, src_slot, slot):
        move = step(PLACE[src_slot], PLACE[slot])
        to_core, crossed = core, 0
        if straight(q, slot):
            to_core = user(slot)
            crossed = jnp.where(core == to_core, 0, 1)
        return remote(
            piece_rows(q, src_slot, half), piece_rows(q, slot, half),
            g_send.at[q, slot], g_recv.at[crossed, q, slot], device(move, to_core),
        )

    def side_copy(q, slot, which):
        piece = piece_rows(q, slot, which)
        return remote(piece, piece, c_send.at[q, slot], g_recv.at[1, q, slot], sibling)

    def to_side(q, slot):
        if slot < 4:
            side_copy(q, slot, half).start()
        elif not straight(q, slot):
            @pl.when(core != user(slot))
            def _():
                side_copy(q, slot, half).start()

    def start_rows(q, slot, children):
        for child in children:
            row_copy(q, slot, child).start()

    def arrive(q, slot):
        children = [[d for d in range(SLOTS) if FROM[q][which][d] == slot] for which in (0, 1)]
        if straight(q, slot):
            @pl.when(core == user(slot))
            def _():
                row_copy(q, OWN, slot).wait_recv()
                start_rows(q, slot, children[user(slot)])
            return
        row_copy(q, OWN, slot).wait_recv()
        if children[0] == children[1]:
            start_rows(q, slot, children[0])
        else:
            for which in (0, 1):
                if children[which]:
                    pl.when(core == which)(lambda: start_rows(q, slot, children[which]))
        to_side(q, slot)

    def side_wait(kind, *slots):
        for slot in slots:
            for q in (2 * kind, 2 * kind + 1):
                if slot < 4:
                    side_copy(q, slot, 128 - half).wait_recv()
                else:
                    @pl.when(core == user(slot))
                    def _(slot=slot, q=q):
                        side_copy(q, slot, 128 - half).wait_recv()

    own_rows = pl.ds(OWN * 256 + half, 128)
    loads[0].wait()
    values = teacher[...].astype(jnp.float32)
    t_rows[own_rows, :] = (
        values / jnp.sqrt(jnp.sum(values * values, axis=1, keepdims=True) + epsilon)
    ).astype(jnp.bfloat16)
    loads[1].wait()
    loads[2].wait()
    student = jnp.dot(features[...], proj[...], preferred_element_type=jnp.float32)
    length = jnp.sqrt(jnp.sum(student * student, axis=1, keepdims=True) + epsilon)
    student = student / length
    unit[...] = student
    norm[...] = jnp.broadcast_to(length, norm.shape)
    s_rows[own_rows, :] = student.astype(jnp.bfloat16)

    pl.semaphore_wait(barrier, len(NEIGHBOURS) + 1)
    for name in FIRST:
        start_rows("TUSV".index(name[0]), OWN, (int(name[1:]),))
    for q in range(4):
        to_side(q, OWN)

    for kind in (T, S):
        top_parts[kind] = jnp.full(top_parts.shape[1:], NEG, jnp.float32)
        sum_parts[kind] = jnp.zeros(sum_parts.shape[1:], jnp.float32)
        col_top[kind] = jnp.full(col_top.shape[1:], NEG, jnp.float32)
        col_sum[kind] = jnp.zeros(col_sum.shape[1:], jnp.float32)

    col_base = 3 + COLS * core
    pair_dims = (((1,), (1,)), ((), ()))
    lanes = lax.broadcasted_iota(jnp.int32, (256, 128), 1)

    def share(j):
        return jnp.where(core == 0, SHARE[0][j], SHARE[1][j]).astype(jnp.float32)

    shares = [share(j) for j in range(COLS)]

    def scores(*pieces):
        def product(kind, a0, na, j):
            buf = rows_buf[kind]
            score_buf[kind][pl.ds(a0 * 256, na * 256), pl.ds(j * 256, 256)] = lax.dot_general(
                buf[pl.ds(a0 * 256, na * 256), :],
                buf[pl.ds(pl.multiple_of((col_base + j) * 256, 256), 256), :],
                pair_dims, preferred_element_type=jnp.float32,
            ) * (logit_scale * log2e)
            if a0 <= 3 < a0 + na and j == 0:
                @pl.when(core == 0)
                def _():
                    tile = score_buf[kind][pl.ds(768, 256), pl.ds(0, 256)]
                    row = lax.broadcasted_iota(jnp.int32, (256, 256), 0)
                    col = lax.broadcasted_iota(jnp.int32, (256, 256), 1)
                    score_buf[kind][pl.ds(768, 256), pl.ds(0, 256)] = jnp.where(row == col, NEG, tile)

        def totals(kind, a0, na, j):
            cols = pl.ds(j * 256, 256)
            for a in range(a0, a0 + na):
                for i in range(4):
                    rows = pl.ds(a * 256 + i * 64, 64)
                    first = score_buf[kind][rows, pl.ds(j * 256, 128)]
                    second = score_buf[kind][rows, pl.ds(j * 256 + 128, 128)]
                    before = top_parts[kind, rows, :]
                    top = jnp.maximum(before, jnp.maximum(first, second))
                    total = jnp.exp2(first - top) + jnp.exp2(second - top)
                    sum_parts[kind, rows, :] = sum_parts[kind, rows, :] * jnp.exp2(before - top) + total * shares[j]
                    top_parts[kind, rows, :] = top
                tile = score_buf[kind][pl.ds(a * 256, 256), cols]
                top = jnp.max(tile, axis=0, keepdims=True)
                total = jnp.sum(jnp.exp2(tile - top), axis=0, keepdims=True)
                col_top[kind, a:a + 1, cols] = top
                col_sum[kind, a:a + 1, cols] = total

        product(*pieces[0])
        for last, piece in zip(pieces, pieces[1:]):
            totals(*last)
            product(*piece)
        totals(*pieces[-1])

    waited = set()

    def tiles(names):
        pieces = []
        for name in names:
            kind, n = "ts".index(name[0]), int(name[1:])
            a0, na, j = (1, 3, n) if n < 4 else (0, 1, n - 4) if n < 8 else (0, 4, 4)
            for slot in (*range(a0, a0 + na), 3 + j, 8 + j):
                if (kind, slot) not in waited:
                    waited.add((kind, slot))
                    side_wait(kind, slot)
            pieces.append((kind, a0, na, j))
        scores(*pieces)

    for upper, names in itertools.groupby(STEPS, str.isupper):
        if upper:
            for name in names:
                arrive("TUSV".index(name[0]), int(name[1:]))
        else:
            tiles(list(names))

    def row_totals(a):
        rows = pl.ds(a * 256, 256)
        packed = jnp.zeros((256, 128), jnp.float32)
        for kind in (T, S):
            parts = top_parts[kind, rows, :]
            top = jnp.max(parts, axis=1, keepdims=True)
            total = jnp.sum(sum_parts[kind, rows, :] * jnp.exp2(parts - top), axis=1, keepdims=True)
            packed = jnp.where(lanes == 2 * kind, top, packed)
            packed = jnp.where(lanes == 2 * kind + 1, total, packed)
        turned = packed.T
        stat_out[a, 0] = turned[0:8, 0:128]
        stat_out[a, 1] = turned[0:8, 128:256]
    def column_totals(j):
        cols = pl.ds(j * 256, 256)
        lines = []
        for kind in (T, S):
            parts = col_top[kind, :, cols]
            top = jnp.max(parts, axis=0, keepdims=True)
            total = jnp.sum(col_sum[kind, :, cols] * jnp.exp2(parts - top), axis=0, keepdims=True)
            lines += [top, total * shares[j]]
        lines.append(jnp.zeros((4, 256), jnp.float32))
        lines = jnp.concatenate(lines, axis=0)
        stat_out[4 + j, 0] = lines[:, 0:128]
        stat_out[4 + j, 1] = lines[:, 128:256]

    def place_at(index, of_core):
        if index < 4:
            return PLACE[index]
        first, second = PLACE[index - 1], PLACE[index + 4]
        return tuple(jnp.where(of_core == 0, p, q) for p, q in zip(first, second))

    def back(move):
        return tuple(4 - m for m in move)

    def stat_copy(index, to_half):
        return remote(
            stat_out.at[index, to_half], stat_in.at[core * 9 + index],
            st_send.at[index * 2 + to_half], st_recv.at[core * 9 + index],
            device(place_at(index, core), to_half),
        )

    def unless_own(index, to_half, action, instead=None):
        if index == 4 and to_half == 1:
            pl.when(core == 0)(action)
            if instead is not None:
                pl.when(core == 1)(instead)
        else:
            action()

    def keep_stat():
        stat_in[9 + 4] = stat_out[4, 1]

    for index in (8, 7, 0, 1, 2, 6, 5, 3, 4):
        if index < 4:
            row_totals(index)
        else:
            column_totals(index - 4)
        for to_half in (0, 1):
            unless_own(index, to_half, lambda: stat_copy(index, to_half).start(), keep_stat)

    def stat_arrival(source):
        return remote(
            stat_out.at[0, 0], stat_in.at[source], st_send.at[0], st_recv.at[source], sibling
        )

    for source in range(18):
        if source == 9 + 4:
            pl.when(core == 0)(lambda: stat_arrival(13).wait_recv())
        else:
            stat_arrival(source).wait_recv()

    lines = []
    for kind in (T, S):
        tops = stat_in[:, 2 * kind, :]
        top = jnp.max(tops, axis=0, keepdims=True)
        total = jnp.sum(stat_in[:, 2 * kind + 1, :] * jnp.exp2(tops - top), axis=0, keepdims=True)
        lines.append(top + jnp.log(total) * log2e)
    lines.append(jnp.zeros((6, 128), jnp.float32))
    lse_out[...] = jnp.concatenate(lines, axis=0)

    def lse_copy(of_core, index):
        return remote(
            lse_out, lse_in.at[index, core],
            l_send.at[of_core * 9 + index], l_recv.at[index * 2 + core],
            device(back(place_at(index, jnp.int32(of_core)) if index < 4 else PLACE[index - 1 + 5 * of_core]), of_core),
        )

    def lse_arrival(index, from_half):
        return remote(
            lse_out, lse_in.at[index, from_half], l_send.at[0], l_recv.at[index * 2 + from_half], sibling
        )

    def keep_lse():
        lse_in[4, 1] = lse_out[...]

    for index in (8, 0, 7, 1, 2, 6, 5, 3, 4):
        for of_core in (0, 1):
            if index == 4 and of_core == 1:
                pl.when(core == 0)(lambda: lse_copy(1, 4).start())
                pl.when(core == 1)(keep_lse)
            else:
                lse_copy(of_core, index).start()
    def roots(i, carry):
        rows = pl.ds(pl.multiple_of(i * 64, 64), 64)
        for score in score_buf:
            score[rows, :] = jnp.exp2(score[rows, :] * 0.5)
        return carry

    lax.fori_loop(0, 16, roots, 0)

    for index in range(9):
        for from_half in (0, 1):
            unless_own(index, from_half, lambda: lse_arrival(index, from_half).wait_recv())

    for a in range(4):
        lines = jnp.concatenate(
            [
                jnp.exp2(-0.5 * jnp.concatenate([lse_in[a, 0], lse_in[a, 1]], axis=1)),
                jnp.zeros((120, 256), jnp.float32),
            ],
            axis=0,
        ).T
        for kind in (T, S):
            lse_rows[kind, pl.ds(a * 256, 256), :] = jnp.broadcast_to(lines[:, kind:kind + 1], (256, 128))

    def square(value):
        return value * value

    def weights(a):
        for j in range(COLS):
            for side in (0, 1):
                col_roots = [jnp.exp2(-0.5 * lse_in[4 + j, side, kind:kind + 1, :]) for kind in (T, S)]
                for i in range(4):
                    rows = pl.ds(a * 256 + i * 64, 64)
                    cols = pl.ds(j * 256 + side * 128, 128)
                    s_tile, t_tile = s_score[rows, cols], t_score[rows, cols]
                    value = (
                        square(s_tile * lse_rows[S, rows, :]) + square(s_tile * col_roots[S])
                        - square(t_tile * lse_rows[T, rows, :]) - square(t_tile * col_roots[T])
                    )
                    weight[rows, cols] = (value * shares[j]).astype(jnp.bfloat16)

    def part_a_copy(a):
        piece = part_a.at[core, a, other]
        return remote(piece, piece, pa_send.at[a], pa_recv.at[a], sibling)

    def part_b_copy(j):
        piece = part_b.at[core, j, other]
        return remote(piece, piece, pb_send.at[j], pb_recv.at[j], sibling)

    def part_a_arrival(a):
        piece = part_a.at[other, a, core]
        return remote(piece, piece, pa_send.at[a], pa_recv.at[a], sibling)

    def part_b_arrival(j):
        piece = part_b.at[other, j, core]
        return remote(piece, piece, pb_send.at[j], pb_recv.at[j], sibling)

    def rows_term(a):
        term = jnp.dot(
            weight[pl.ds(a * 256, 256), :],
            s_rows[pl.ds(pl.multiple_of(col_base * 256, 256), COLS * 256), :],
            preferred_element_type=jnp.float32,
        ).astype(jnp.bfloat16)
        part_a[core, a] = term.reshape(2, 128, 1024)

    def columns_term(j):
        term = lax.dot_general(
            weight[:, pl.ds(j * 256, 256)], s_rows[pl.ds(0, 1024), :],
            (((0,), (0,)), ((), ())), preferred_element_type=jnp.float32,
        ).astype(jnp.bfloat16)
        part_b[core, j] = term.reshape(2, 128, 1024)
        part_b_copy(j).start()

    def piece_of(ref, piece):
        return ref.at[pl.ds(piece * 64, 64), :]

    def slot_ready(slot):
        if slot < 4:
            part_a_arrival(slot).wait_recv()
        if slot >= 3:
            @pl.when(core != (slot - 3) // 5)
            def _():
                part_b_arrival((slot - 3) % 5).wait_recv()

    def sum_copy(which, slot, piece, src):
        into = INTO[which][piece][slot]
        return remote(
            piece_of(src, piece), piece_of(stage.at[slot], piece),
            r_send.at[slot * 2 + piece], r_recv.at[slot * 2 + piece],
            device(step(PLACE[slot], PLACE[into]), core),
        )

    def slot_terms(which, slot, piece):
        terms = []
        if slot < 4:
            terms += [part_a.at[0, slot, core], part_a.at[1, slot, core]]
        if slot >= 3:
            terms.append(part_b.at[(slot - 3) // 5, (slot - 3) % 5, core])
        for child in range(SLOTS):
            if INTO[which][piece][child] == slot:
                sum_copy(which, child, piece, stage.at[child]).wait_recv()
                terms.append(stage.at[child])
        return terms

    def added(terms, piece):
        return functools.reduce(
            lambda p, q: p + q, [piece_of(term, piece)[...].astype(jnp.float32) for term in terms]
        )

    def send_sum(slot, *pieces):
        def send(which):
            for piece in pieces:
                terms = slot_terms(which, slot, piece)
                if len(terms) == 1:
                    sum_copy(which, slot, piece, terms[0]).start()
                else:
                    piece_of(joined.at[slot], piece)[...] = added(terms, piece).astype(jnp.bfloat16)
                    sum_copy(which, slot, piece, joined.at[slot]).start()

        routes = [
            [(INTO[which][piece][slot], [c for c in range(SLOTS) if INTO[which][piece][c] == slot]) for piece in pieces]
            for which in (0, 1)
        ]
        if routes[0] == routes[1]:
            send(0)
        else:
            pl.when(core == 0)(lambda: send(0))
            pl.when(core == 1)(lambda: send(1))

    ready = set()
    for at, name in enumerate(ORDER):
        if name[0] == "W":
            weights(int(name[1:]))
            if ORDER[at - 1][0] == "A":
                part_a_copy(int(ORDER[at - 1][1:])).start()
        elif name[0] == "A":
            rows_term(int(name[1:]))
            if ORDER[at + 1][0] != "W":
                part_a_copy(int(name[1:])).start()
        elif name[0] == "B":
            columns_term(int(name[1:]))
        else:
            slot, piece = (int(n) for n in name.split("."))
            if slot not in ready:
                ready.add(slot)
                slot_ready(slot)
            send_sum(slot, piece)
    slot_ready(OWN)

    for piece in (0, 1):
        rows = pl.ds(piece * 64, 64)
        grad = logit_scale * added(slot_terms(0, OWN, piece), piece)
        student = unit[rows, :]
        along = jnp.sum(student * grad, axis=1, keepdims=True)
        out[rows, :] = ((grad - student * along) / norm[rows, 0:1]).astype(jnp.bfloat16)

    for kind in range(4):
        for slot in range(SLOTS):
            if slot != OWN:
                row_copy(kind, OWN, slot).wait_send()
            if slot < 4:
                side_copy(kind, slot, half).wait_send()
            elif not straight(kind, slot):
                @pl.when(core != user(slot))
                def _(kind=kind, slot=slot):
                    side_copy(kind, slot, half).wait_send()
    for index in range(9):
        for to_half in (0, 1):
            unless_own(index, to_half, lambda: stat_copy(index, to_half).wait_send())
        for of_core in (0, 1):
            if index == 4 and of_core == 1:
                pl.when(core == 0)(lambda: lse_copy(1, 4).wait_send())
            else:
                lse_copy(of_core, index).wait_send()
    for a in range(4):
        part_a_copy(a).wait_send()
    for j in range(COLS):
        part_b_copy(j).wait_send()
    for slot in range(SLOTS):
        if slot != OWN:
            for piece in (0, 1):
                sum_copy(0, slot, piece, joined.at[slot]).wait_send()


def per_device(features, teacher, proj):
    bf16, f32 = jnp.bfloat16, jnp.float32
    vmem = pl.BlockSpec(memory_space=pltpu.VMEM)
    dma = pltpu.SemaphoreType.DMA
    d_student = pl.pallas_call(
        kernel,
        out_shape=jax.ShapeDtypeStruct((128, 1024), bf16),
        in_specs=[pl.BlockSpec(memory_space=pl.ANY)] * 3,
        out_specs=vmem,
        scratch_shapes=[
            pltpu.VMEM((128, 1024), bf16),
            pltpu.VMEM((128, 1024), bf16),
            pltpu.VMEM((1024, 1024), bf16),
            pltpu.VMEM((SLOTS * 256, 1024), bf16),
            pltpu.VMEM((SLOTS * 256, 1024), bf16),
            pltpu.VMEM((1024, COLS * 256), f32),
            pltpu.VMEM((1024, COLS * 256), f32),
            pltpu.VMEM((1024, COLS * 256), bf16),
            pltpu.VMEM((2, 1024, 128), f32),
            pltpu.VMEM((2, 1024, 128), f32),
            pltpu.VMEM((2, 8, COLS * 256), f32),
            pltpu.VMEM((2, 8, COLS * 256), f32),
            pltpu.VMEM((9, 2, 8, 128), f32),
            pltpu.VMEM((18, 8, 128), f32),
            pltpu.VMEM((8, 128), f32),
            pltpu.VMEM((9, 2, 8, 128), f32),
            pltpu.VMEM((2, 1024, 128), f32),
            pltpu.VMEM((2, 4, 2, 128, 1024), bf16),
            pltpu.VMEM((2, COLS, 2, 128, 1024), bf16),
            pltpu.VMEM((SLOTS, 128, 1024), bf16),
            pltpu.VMEM((SLOTS, 128, 1024), bf16),
            pltpu.VMEM((128, 1024), f32),
            pltpu.VMEM((128, 128), f32),
            dma((4, SLOTS)), dma((2, 4, SLOTS)), dma((4, SLOTS)),
            dma((18,)), dma((18,)), dma((18,)), dma((18,)),
            dma((4,)), dma((4,)), dma((COLS,)), dma((COLS,)), dma((2 * SLOTS,)), dma((2 * SLOTS,)), dma((3,)),
        ],
        compiler_params=pltpu.CompilerParams(
            collective_id=0, has_side_effects=True, vmem_limit_bytes=60 * 2**20
        ),
        cost_estimate=pl.CostEstimate(flops=9_000_000_000, bytes_accessed=4_000_000, transcendentals=9_000_000),
    )(features, teacher, proj)
    return lax.dot_general(
        d_student, proj, (((1,), (1,)), ((), ())), preferred_element_type=f32
    )


def solution(mesh):
    in_specs = (P(("sub", "dp", "mp"), None), P(("sub", "dp", "mp"), None), P())
    out_specs = P(("sub", "dp", "mp"), None)
    return jax.shard_map(
        per_device, mesh=mesh, in_specs=in_specs, out_specs=out_specs, check_vma=False
    )
```
